32 devices in a mesh: row: 8 (over z, x), col: 4 (over y, core).
Axes of the slice: x: 2, y: 2, z: 4, core: 2. Of those that a mesh axis runs over, the one named last changes fastest.
Arguments:
- object_field: float32 [2, 4096, 1536], P(None, 'row', 'col'), may hold values from -6 to 6
- probe_field: float32 [2, 256, 256], replicated, may hold values from -6 to 6
- amplitudes: bfloat16 [2, 384, 256, 256], P(None, ('row', 'col')), may hold values from 0.29882812 to 3
- positions: int32 [2, 2, 384], P(None, None, ('row', 'col')), may hold values from 0 to 511, as said below
- live_counts: int32 [2, 4, 8], P(None, 'col', 'row'), may hold values from 1 to 12, 24 in all within a row
Outputs:
- object_out: float32 [2, 4096, 1536], P(None, 'row', 'col')
- probe_out: float32 [2, 256, 256], replicated
The draws below stay inside these ranges and needn't reach their ends.
Inputs may be any that keep to these rules, and one draw needn't show every extreme that they name: `positions`: every offset is below 512 for rows and below 384 for columns; in the last block row the row offset is at most 256, in the last block column the column offset at most 128, so every patch lies inside the object. The live frames of a device are its first slots. For every iteration t and block column c, the 8 counts live_counts[t, c, :] of that block column's devices sum to 24, and one of them is 12; no such sum holds over the devices of a block row.
All inputs are finite; a program needn't handle non-finite values.
Results may differ from the reference program's by a relative error of at most 0.0019.
Values may be sent and summed in bfloat16 or wider, within the bound.
A program may use at most 128 MiB of HBM per device.

```python
import math
import jax
import jax.numpy as jnp
import numpy as np
from jax import lax

FRAME = 256
TILE_ROWS = 512
TILE_COLS = 384
BATCH_DEV = 3
ITERS = 2
FRAMES_DEV = 12
FRAMES = 384
ROWS = 4096
COLS = 1536
N_ROW = 8
N_COL = 4
DEVICES = 32


def draw_positions(key, part):
    frame_ids = jnp.arange(FRAMES, dtype=jnp.int32)
    device_ids = frame_ids // FRAMES_DEV
    row_ids = device_ids // N_COL
    col_ids = device_ids % N_COL
    row_high = jnp.where(row_ids == N_ROW - 1, TILE_ROWS - FRAME + 1, TILE_ROWS).astype(jnp.int32)
    col_high = jnp.where(col_ids == N_COL - 1, TILE_COLS - FRAME + 1, TILE_COLS).astype(jnp.int32)
    key_rows = jax.random.fold_in(key, 11)
    key_columns = jax.random.fold_in(key, 23)
    row_draw = jax.random.randint(key_rows, (ITERS, FRAMES), 0, row_high[None, :], dtype=jnp.int32)
    col_draw = jax.random.randint(key_columns, (ITERS, FRAMES), 0, col_high[None, :], dtype=jnp.int32)
    return jnp.stack([row_draw, col_draw], axis=1)


def block_levels(rng, extent, pieces, least, top_value):
    def one(dim, blocks):
        draws = jax.random.uniform(jax.random.fold_in(jax.random.fold_in(rng, 6), dim), (blocks,), jnp.float32, least / len(pieces), top_value / len(pieces))
        return jnp.repeat(jnp.exp(draws), extent[dim] // blocks).reshape((-1,) + (1,) * (len(extent) - dim - 1))

    level = one(*pieces[0])
    for cut in pieces[1:]:
        level = level * one(*cut)
    return level


def split_up(count, total, reach, slope):
    weights = [(1 << 20) // math.isqrt(standing ** slope) + 1 for standing in range(2, count + 1)]
    spare, holding = total - reach - (count - 1), [1] * (count - 1)
    while spare > 0:
        movable = [i for i in range(count - 1) if holding[i] < reach]
        mass, budget = sum([weights[i] for i in movable]), spare
        for i in movable:
            extra = min(reach - holding[i], max(1, budget * weights[i] // mass), spare)
            holding[i] = holding[i] + extra
            spare = spare - extra
    return np.array([reach] + holding)


def uneven_parts(key, number_of, total, limit, skew):
    if number_of == 2:
        one = jax.random.randint(key, (), max(1, total - limit), min(limit, total - 1) + 1)
        return jnp.stack([one, total - one])
    sizes = jnp.asarray(split_up(number_of, total, limit, skew), jnp.int32)
    twos = (number_of - 1) // 2
    giver, receiver = sizes[1:1 + 2 * twos:2], sizes[2:2 + 2 * twos:2]
    slack = jnp.minimum(giver - 1, limit - receiver)
    passed = jax.random.randint(jax.random.fold_in(key, 1), (twos,), 0, 1 << 20) % (slack + 1)
    sizes = sizes.at[1:1 + 2 * twos:2].set(giver - passed).at[2:2 + 2 * twos:2].set(receiver + passed)
    return sizes[jax.random.permutation(jax.random.fold_in(key, 2), number_of)]


def scatter_about(own_key, extent, scale, bound, cuts=(), kind=jnp.bfloat16):
    level = block_levels(own_key, extent, cuts, -0.22, 0.18) if cuts else 1.0
    array = jax.random.normal(own_key, extent, jnp.float32) * scale * level
    return jnp.minimum(jnp.maximum(array, -bound), bound).astype(kind)


def setup_inputs(seed: int = 0) -> dict:
    key_list = jax.random.split(jax.random.key(seed), 6)
    return {
        "object_field": scatter_about(key_list[0], (2, ROWS, COLS), 1.0, 6.0, ((1, 8), (2, 4)), jnp.float32),
        "probe_field": scatter_about(key_list[1], (2, FRAME, FRAME), 1.0, 6.0, (), jnp.float32),
        "amplitudes": jnp.clip(jnp.exp(math.log(3.0) - 2.306499 * jax.random.uniform(key_list[2], (ITERS, FRAMES, FRAME, FRAME), jnp.float32) ** block_levels(key_list[2], (ITERS, FRAMES, FRAME, FRAME), ((1, 32),), -0.2, 0.2)), 0.29882812, 3.0).astype(jnp.bfloat16),
        "positions": draw_positions(jax.random.fold_in(key_list[5], 71), 0),
        "live_counts": jax.vmap(lambda own: uneven_parts(own, N_ROW, N_ROW * BATCH_DEV, FRAMES_DEV, 2))(jax.random.split(key_list[4], ITERS * N_COL)).reshape((ITERS, N_COL, N_ROW)).astype(jnp.int32),
    }


FLOOR = 0.3
ALPHA = 0.5

def chirp_tables(frame_size):
    offset = jnp.arange(frame_size, dtype=jnp.int32)
    differ = offset[:, None] - offset[None, :]
    phase_units = differ * differ % (2 * frame_size)
    phase = jnp.pi * phase_units.astype(jnp.float32) / frame_size
    scale = 1.0 / math.sqrt(frame_size)
    return ((jnp.cos(phase) * scale).astype(jnp.bfloat16), (jnp.sin(phase) * scale).astype(jnp.bfloat16))

def left_product(real_table, imag_table, real_part, imag_part):

    def product(table, part):
        return jnp.einsum('ab,nbc->nac', table.astype(jnp.float32), part.astype(jnp.float32))
    return (product(real_table, real_part) - product(imag_table, imag_part), product(real_table, imag_part) + product(imag_table, real_part))

def right_product(real_table, imag_table, real_part, imag_part):

    def product(part, table):
        return jnp.einsum('nab,bc->nac', part.astype(jnp.float32), table.astype(jnp.float32))
    return (product(real_part, real_table) - product(imag_part, imag_table), product(imag_part, real_table) + product(real_part, imag_table))

def frame_terms(patches, frame_amps, probe_field, real_table, imag_table, weights):
    probe_real, probe_imag = (probe_field[0], probe_field[1])
    patch_real = patches[:, 0].astype(jnp.float32)
    patch_imag = patches[:, 1].astype(jnp.float32)
    wave_real = (probe_real * patch_real - probe_imag * patch_imag).astype(jnp.bfloat16)
    wave_imag = (probe_real * patch_imag + probe_imag * patch_real).astype(jnp.bfloat16)
    near_real, near_imag = left_product(real_table, imag_table, wave_real, wave_imag)
    near_real, near_imag = (near_real.astype(jnp.bfloat16), near_imag.astype(jnp.bfloat16))
    far_real, far_imag = right_product(real_table, imag_table, near_real, near_imag)
    magnitude = jnp.sqrt(far_real * far_real + far_imag * far_imag)
    factor = 1.0 - frame_amps.astype(jnp.float32) / jnp.maximum(magnitude, FLOOR)
    misfit_real = (far_real * factor).astype(jnp.bfloat16)
    misfit_imag = (far_imag * factor).astype(jnp.bfloat16)
    conj_table = -imag_table
    back_real, back_imag = left_product(real_table, conj_table, misfit_real, misfit_imag)
    back_real, back_imag = (back_real.astype(jnp.bfloat16), back_imag.astype(jnp.bfloat16))
    update_real, update_imag = right_product(real_table, conj_table, back_real, back_imag)
    weight_col = weights[:, None, None]
    grad_real = (probe_real * update_real + probe_imag * update_imag) * weight_col
    grad_imag = (probe_real * update_imag - probe_imag * update_real) * weight_col
    gradients = jnp.stack([grad_real, grad_imag], axis=1).astype(jnp.bfloat16)
    probe_real_term = lax.optimization_barrier(jnp.sum(weight_col * (patch_real * update_real + patch_imag * update_imag), axis=0))
    probe_imag_term = lax.optimization_barrier(jnp.sum(weight_col * (patch_real * update_imag - patch_imag * update_real), axis=0))
    weight_term = lax.optimization_barrier(jnp.sum(weight_col * (patch_real * patch_real + patch_imag * patch_imag), axis=0))
    return (gradients, jnp.stack([probe_real_term, probe_imag_term], axis=0), weight_term)

def reference(object_field, probe_field, amplitudes, positions, live_counts):
    real_table, imag_table = chirp_tables(FRAME)
    frame_ids = jnp.arange(FRAMES, dtype=jnp.int32)
    device_ids = frame_ids // FRAMES_DEV
    slot_ids = frame_ids % FRAMES_DEV
    row_ids = device_ids // N_COL
    col_ids = device_ids % N_COL
    anchor = jnp.zeros((), jnp.int32)
    live_total = DEVICES * BATCH_DEV
    for iteration in range(ITERS):
        counts = live_counts[iteration][col_ids, row_ids]
        chosen = jnp.nonzero(slot_ids < counts, size=live_total)[0].astype(jnp.int32)
        top_rows = (row_ids[chosen] * TILE_ROWS + positions[iteration, 0][chosen]).astype(jnp.int32)
        left_columns = (col_ids[chosen] * TILE_COLS + positions[iteration, 1][chosen]).astype(jnp.int32)
        chosen_amps = amplitudes[iteration][chosen]

        def block_terms(block):
            block_tops, block_lefts, block_amps = block

            def cut_patch(top_row, left_column):
                return lax.dynamic_slice(object_field, (anchor, top_row, left_column), (2, FRAME, FRAME))
            patches = jax.vmap(cut_patch)(block_tops, block_lefts).astype(jnp.bfloat16)
            return frame_terms(patches, block_amps, probe_field, real_table, imag_table, jnp.ones((BATCH_DEV,), jnp.float32))
        gradients, probe_terms, weight_terms = lax.map(block_terms, (top_rows.reshape(DEVICES, BATCH_DEV), left_columns.reshape(DEVICES, BATCH_DEV), chosen_amps.reshape(DEVICES, BATCH_DEV, FRAME, FRAME)))
        flat_grads = gradients.reshape(live_total, 2, FRAME, FRAME)

        def add_patch(index, total):
            corner = (anchor, top_rows[index], left_columns[index])
            current = lax.dynamic_slice(total, corner, (2, FRAME, FRAME))
            return lax.dynamic_update_slice(total, current + flat_grads[index].astype(jnp.float32), corner)
        object_sum = lax.fori_loop(0, live_total, add_patch, jnp.zeros_like(object_field))
        probe_sum = lax.optimization_barrier(jnp.sum(probe_terms, axis=0))
        weight_sum = lax.optimization_barrier(jnp.sum(weight_terms, axis=0))
        step_size = ALPHA / (jnp.max(probe_field[0] * probe_field[0] + probe_field[1] * probe_field[1]) + 1e-06)
        object_field = object_field - step_size * object_sum
        probe_field = probe_field - probe_sum / (weight_sum + 1.0)
    return (object_field, probe_field)
```

```python
import functools
import math

import jax
import jax.numpy as jnp
import ml_dtypes
import numpy as np
from jax import lax
from jax.experimental import pallas as pl
from jax.experimental.pallas import tpu as pltpu
from jax.sharding import PartitionSpec as P

ITERS = 2


FLOOR = 0.3
ALPHA = 0.5
LANES = 128
SUBLANES = 8
MESH = pl.DeviceIdType.MESH


def passed_along(value, axis, steps):
    count = lax.axis_size(axis)
    first, last = (max(0, -steps), min(count, count - steps))
    return lax.ppermute(value, axis, [(source, source + steps) for source in range(first, last)])


def chirp_blocks(frame_size):
    offset = np.arange(frame_size, dtype=np.int32)
    differ = offset[:, None] - offset[None, :]
    phase = np.pi * (differ * differ % (2 * frame_size)).astype(np.float64) / frame_size
    scale = 1.0 / math.sqrt(frame_size)
    real, imag = (np.cos(phase) * scale, np.sin(phase) * scale)
    forward = np.block([[real, -imag], [imag, real]]).astype(ml_dtypes.bfloat16)
    return jnp.asarray(forward), jnp.asarray(forward.T.copy())


def frames_kernel(
    positions, live, extended, probe, amplitudes, left_table, right_table, gathered, sums
):
    size = probe.shape[-1]
    halves = size // LANES
    gathered[...] = jnp.zeros_like(gathered)
    sums[...] = jnp.zeros_like(sums)
    groups = size // SUBLANES
    lane = lax.broadcasted_iota(jnp.int32, (groups + 1, SUBLANES, LANES), 2)
    sublane = lax.broadcasted_iota(jnp.int32, (groups, SUBLANES, LANES), 1)

    def dot(a, b):
        return jnp.dot(a, b, preferred_element_type=jnp.float32)

    def one_frame(slot, weight):
        top = positions[0, slot]
        left = positions[1, slot]
        block = left // LANES
        shift = left - block * LANES
        row_block = top // SUBLANES
        row_shift = top - row_block * SUBLANES
        rows = pl.ds(row_block, groups + 1)

        def columns(part):
            return pl.ds(pl.multiple_of((block + part) * LANES, LANES), LANES)

        patch = []
        back_shift = lax.rem(LANES - shift, LANES)
        back_row_shift = lax.rem(SUBLANES - row_shift, SUBLANES)
        keep = lane < LANES - shift
        keep_rows = sublane < SUBLANES - row_shift
        for comp in range(2):
            turned = [
                pltpu.roll(extended[comp, rows, :, columns(part)], back_shift, 2)
                for part in range(halves + 1)
            ]
            picked = []
            for part in range(halves):
                tall = pltpu.roll(
                    jnp.where(keep, turned[part], turned[part + 1]), back_row_shift, 1
                )
                picked.append(
                    jnp.where(keep_rows, tall[:groups], tall[1:]).reshape(size, LANES)
                )
            patch.append(
                jnp.concatenate(picked, axis=1).astype(jnp.bfloat16).astype(jnp.float32)
            )
        patch_real, patch_imag = patch
        probe_real, probe_imag = probe[0], probe[1]
        wave = jnp.concatenate(
            [
                probe_real * patch_real - probe_imag * patch_imag,
                probe_real * patch_imag + probe_imag * patch_real,
            ],
            axis=0,
        ).astype(jnp.bfloat16)
        near = dot(left_table[...], wave).astype(jnp.bfloat16)
        far = dot(jnp.concatenate([near[:size], near[size:]], axis=1), right_table[...])
        far_real, far_imag = far[:, :size], far[:, size:]
        power = far_real * far_real + far_imag * far_imag
        factor = 1.0 - amplitudes[slot].astype(jnp.float32) * lax.rsqrt(
            jnp.maximum(power, FLOOR * FLOOR)
        )
        misfit = jnp.concatenate([far_real * factor, far_imag * factor], axis=0).astype(
            jnp.bfloat16
        )
        back = dot(right_table[...], misfit).astype(jnp.bfloat16)
        update = dot(jnp.concatenate([back[:size], back[size:]], axis=1), left_table[...])
        update_real, update_imag = update[:, :size] * weight, update[:, size:] * weight
        terms = (
            patch_real * update_real + patch_imag * update_imag,
            patch_real * update_imag - patch_imag * update_real,
            (patch_real * patch_real + patch_imag * patch_imag) * weight,
        )
        for comp, term in enumerate(terms):
            for half in range(halves):
                sums[comp * halves + half] += term[:, half * LANES : (half + 1) * LANES]
        grads = (
            probe_real * update_real + probe_imag * update_imag,
            probe_real * update_imag - probe_imag * update_real,
        )
        moved = lane >= shift
        moved_rows = sublane >= row_shift
        for comp, grad in enumerate(grads):
            grad = grad.astype(jnp.bfloat16).astype(jnp.float32)
            turned = []
            for half in range(halves):
                tall = pltpu.roll(
                    grad[:, half * LANES : (half + 1) * LANES].reshape(groups, SUBLANES, LANES),
                    row_shift,
                    1,
                )
                tall = jnp.concatenate(
                    [
                        jnp.where(moved_rows[:1], tall[:1], 0.0),
                        jnp.where(moved_rows[1:], tall[1:], tall[:-1]),
                        jnp.where(moved_rows[:1], 0.0, tall[-1:]),
                    ],
                    axis=0,
                )
                turned.append(pltpu.roll(tall, shift, 2))
            nothing = jnp.zeros_like(turned[0])
            before = [nothing] + turned
            after = turned + [nothing]
            for part in range(halves + 1):
                gathered[comp, rows, :, columns(part)] += jnp.where(
                    moved, after[part], before[part]
                )

    count = live[0]

    def pair(index, carry):
        one_frame(2 * index, jnp.float32(1.0))
        one_frame(2 * index + 1, (2 * index + 1 < count).astype(jnp.float32))
        return carry

    lax.fori_loop(0, (count + 1) // 2, pair, 0)


def frame_sums(extended, probe_field, amplitudes, positions, live, tables):
    size = probe_field.shape[-1]
    slots = amplitudes.shape[0]
    vmem = pl.BlockSpec(memory_space=pltpu.VMEM)
    smem = pl.BlockSpec(memory_space=pltpu.SMEM)
    planes, tall, width = extended.shape
    extended = extended.reshape(planes, tall // SUBLANES, SUBLANES, width)
    gathered, sums = pl.pallas_call(
        frames_kernel,
        out_shape=(
            jax.ShapeDtypeStruct(extended.shape, jnp.float32),
            jax.ShapeDtypeStruct((3 * size // LANES, size, LANES), jnp.float32),
        ),
        in_specs=[smem, smem] + [vmem] * 5,
        out_specs=(vmem, vmem),
        compiler_params=pltpu.CompilerParams(vmem_limit_bytes=48 * 1024 * 1024),
        cost_estimate=pl.CostEstimate(
            flops=slots * 32 * size**3,
            bytes_accessed=12 * 1024 * 1024,
            transcendentals=slots * size * size,
        ),
        name="frames",
    )(positions, live, extended, probe_field, amplitudes, *tables)
    return gathered.reshape(planes, tall, width), sums


def probe_kernel(
    n_row,
    n_col,
    sums,
    probe,
    out,
    wide,
    got_col,
    own_rows,
    got_row,
    piece,
    steps,
    joined,
    got_steps,
    col_send,
    col_recv,
    row_send,
    row_recv,
    back_row_send,
    back_row_recv,
    back_col_send,
    back_col_recv,
):
    row, col = lax.axis_index("row"), lax.axis_index("col")
    planes, size, _ = sums.shape
    chunk = size // n_col
    part = chunk // n_row
    comps = planes * 2 // 3

    def along_col(step):
        return (row, lax.rem(col + step, n_col))

    def along_row(step):
        return (lax.rem(row + step, n_row), col)

    barrier = pltpu.get_barrier_semaphore()
    for step in range(1, n_col):
        pl.semaphore_signal(barrier, inc=1, device_id=along_col(step), device_id_type=MESH)
    for step in range(1, n_row):
        pl.semaphore_signal(barrier, inc=1, device_id=along_row(step), device_id_type=MESH)
    wide[...] = sums[...].astype(jnp.bfloat16)
    pl.semaphore_wait(barrier, n_col + n_row - 2)

    def remote(source, target, send, recv, device):
        copy = pltpu.make_async_remote_copy(
            src_ref=source,
            dst_ref=target,
            send_sem=send,
            recv_sem=recv,
            device_id=device,
            device_id_type=MESH,
        )
        copy.start()
        return copy

    def rows_of(index, length):
        return pl.ds(pl.multiple_of(index * length, length), length)

    first = []
    for step in range(1, n_col):
        their = lax.rem(col + step, n_col)
        first.append(
            remote(
                wide.at[:, rows_of(their, chunk), :],
                got_col.at[step - 1],
                col_send.at[step - 1],
                col_recv.at[step - 1],
                along_col(step),
            )
        )
    total = sums[:, rows_of(col, chunk), :]
    for step, copy in enumerate(first):
        copy.wait_recv()
        total = total + got_col[step].astype(jnp.float32)
    for index in range(n_row):
        own_rows[index] = total[:, index * part : (index + 1) * part, :]
    second = []
    for step in range(1, n_row):
        their = lax.rem(row + step, n_row)
        second.append(
            remote(
                own_rows.at[their],
                got_row.at[step - 1],
                row_send.at[step - 1],
                row_recv.at[step - 1],
                along_row(step),
            )
        )
    total = own_rows[row]
    for step, copy in enumerate(second):
        copy.wait_recv()
        total = total + got_row[step]
    halves = planes // 3
    weight = total[2 * halves :] + 1.0
    piece[...] = jnp.concatenate(
        [total[:halves] / weight, total[halves : 2 * halves] / weight], axis=0
    )
    third = [
        remote(
            piece,
            steps.at[row],
            back_row_send.at[step - 1],
            back_row_recv.at[step - 1],
            along_row(step),
        )
        for step in range(1, n_row)
    ]
    steps[row] = piece[...]
    for copy in third:
        copy.wait_recv()
    joined[...] = jnp.concatenate([steps[index] for index in range(n_row)], axis=1)
    fourth = [
        remote(
            joined,
            got_steps.at[col],
            back_col_send.at[step - 1],
            back_col_recv.at[step - 1],
            along_col(step),
        )
        for step in range(1, n_col)
    ]
    got_steps[col] = joined[...]
    for copy in fourth:
        copy.wait_recv()
    for index in range(n_col):
        rows = slice(index * chunk, (index + 1) * chunk)
        for plane in range(comps):
            comp, half = divmod(plane, halves)
            lanes = slice(half * LANES, (half + 1) * LANES)
            out[comp, rows, lanes] = probe[comp, rows, lanes] - got_steps[index, plane]
    for copy in first + second + third + fourth:
        copy.wait_send()


def next_probe(sums, probe_field):
    n_row, n_col = lax.axis_size("row"), lax.axis_size("col")
    planes, size, _ = sums.shape
    chunk = size // n_col
    part = chunk // n_row
    comps = planes * 2 // 3
    vmem = pl.BlockSpec(memory_space=pltpu.VMEM)
    dma = pltpu.SemaphoreType.DMA
    return pl.pallas_call(
        functools.partial(probe_kernel, n_row, n_col),
        out_shape=jax.ShapeDtypeStruct(probe_field.shape, jnp.float32),
        in_specs=[vmem, vmem],
        out_specs=vmem,
        scratch_shapes=[
            pltpu.VMEM(sums.shape, jnp.bfloat16),
            pltpu.VMEM((n_col - 1, planes, chunk, LANES), jnp.bfloat16),
            pltpu.VMEM((n_row, planes, part, LANES), jnp.float32),
            pltpu.VMEM((n_row - 1, planes, part, LANES), jnp.float32),
            pltpu.VMEM((comps, part, LANES), jnp.float32),
            pltpu.VMEM((n_row, comps, part, LANES), jnp.float32),
            pltpu.VMEM((comps, chunk, LANES), jnp.float32),
            pltpu.VMEM((n_col, comps, chunk, LANES), jnp.float32),
            dma((n_col - 1,)),
            dma((n_col - 1,)),
            dma((n_row - 1,)),
            dma((n_row - 1,)),
            dma((n_row - 1,)),
            dma((n_row - 1,)),
            dma((n_col - 1,)),
            dma((n_col - 1,)),
        ],
        compiler_params=pltpu.CompilerParams(
            collective_id=0, has_side_effects=True, vmem_limit_bytes=32 * 1024 * 1024
        ),
        cost_estimate=pl.CostEstimate(
            flops=planes * size * LANES * 4, bytes_accessed=4 * 1024 * 1024, transcendentals=0
        ),
        name="probe_sum",
    )(sums, probe_field)


def extend_block(object_field, frame_size):
    below = passed_along(object_field[:, :frame_size, :].astype(jnp.bfloat16), "row", -1)
    taller = jnp.concatenate([object_field[:, :, :frame_size].astype(jnp.bfloat16), below[:, :, :frame_size]], axis=1)
    beside = passed_along(taller, "col", -1).astype(jnp.float32)
    own = jnp.concatenate([object_field, below.astype(jnp.float32)], axis=1)
    return jnp.concatenate([own, beside], axis=2)


def fold_rims(gathered, block_rows, block_columns):
    from_left = passed_along(gathered[:, :, block_columns:].astype(jnp.bfloat16), "col", 1).astype(
        jnp.float32
    )
    narrow = gathered[:, :, :block_columns]
    narrow = narrow.at[:, :, : from_left.shape[2]].add(from_left)
    from_above = passed_along(narrow[:, block_rows:, :].astype(jnp.bfloat16), "row", 1).astype(
        jnp.float32
    )
    return narrow[:, :block_rows, :].at[:, : from_above.shape[1], :].add(from_above)


def local(object_field, probe_field, amplitudes, positions, live_counts):
    frame_size = probe_field.shape[-1]
    block_rows, block_columns = (object_field.shape[1], object_field.shape[2])
    tables = chirp_blocks(frame_size)
    for iteration in range(ITERS):
        extended = extend_block(object_field, frame_size)
        gathered, sums = frame_sums(
            extended,
            probe_field,
            amplitudes[iteration],
            positions[iteration],
            live_counts[iteration, 0],
            tables,
        )
        object_sum = fold_rims(gathered, block_rows, block_columns)
        step_size = ALPHA / (
            jnp.max(probe_field[0] * probe_field[0] + probe_field[1] * probe_field[1]) + 1e-06
        )
        object_field = object_field - step_size * object_sum
        probe_field = next_probe(sums, probe_field)
    return (object_field, probe_field)


def solution(mesh):
    placed = (
        P(None, "row", "col"),
        P(),
        P(None, ("row", "col"), None, None),
        P(None, None, ("row", "col")),
        P(None, "col", "row"),
    )
    return jax.shard_map(
        local, mesh=mesh, in_specs=placed, out_specs=(P(None, "row", "col"), P()), check_vma=False
    )
```

```python
import functools
import math

import jax
import jax.numpy as jnp
import ml_dtypes
import numpy as np
from jax import lax
from jax.experimental import pallas as pl
from jax.experimental.pallas import tpu as pltpu
from jax.sharding import PartitionSpec as P

ITERS = 2


FLOOR = 0.3
ALPHA = 0.5
LANES = 128
SUBLANES = 8
MESH = pl.DeviceIdType.MESH


def chirp_blocks(frame_size):
    offset = np.arange(frame_size, dtype=np.int32)
    differ = offset[:, None] - offset[None, :]
    phase = np.pi * (differ * differ % (2 * frame_size)).astype(np.float64) / frame_size
    scale = 1.0 / math.sqrt(frame_size)
    real, imag = (np.cos(phase) * scale, np.sin(phase) * scale)
    forward = np.block([[real, -imag], [imag, real]]).astype(ml_dtypes.bfloat16)
    return jnp.asarray(forward), jnp.asarray(forward.T.copy())


def frames_kernel(
    positions,
    live,
    block,
    below,
    beside,
    corner,
    probe,
    amplitudes,
    left_table,
    right_table,
    own_grad,
    below_grad,
    beside_grad,
    corner_grad,
    sums,
    extended,
    gathered,
):
    size = probe.shape[-1]
    halves = size // LANES
    block_rows, block_columns = block.shape[1:]
    regions = (
        (block, own_grad, slice(0, block_rows), slice(0, block_columns)),
        (below, below_grad, slice(block_rows, None), slice(0, block_columns)),
        (beside, beside_grad, slice(0, block_rows), slice(block_columns, None)),
        (corner, corner_grad, slice(block_rows, None), slice(block_columns, None)),
    )

    def grouped(rows):
        stop = None if rows.stop is None else rows.stop // SUBLANES
        return slice(rows.start // SUBLANES, stop)

    for source, _, rows, lanes in regions:
        planes, tall, width = source.shape
        extended[:, grouped(rows), :, lanes] = (
            source[...].astype(jnp.float32).reshape(planes, tall // SUBLANES, SUBLANES, width)
        )
    gathered[...] = jnp.zeros_like(gathered)
    sums[...] = jnp.zeros_like(sums)
    groups = size // SUBLANES
    lane = lax.broadcasted_iota(jnp.int32, (groups + 1, SUBLANES, LANES), 2)
    sublane = lax.broadcasted_iota(jnp.int32, (groups, SUBLANES, LANES), 1)

    def dot(a, b):
        return jnp.dot(a, b, preferred_element_type=jnp.float32)

    def one_frame(slot, weight):
        top = positions[0, slot]
        left = positions[1, slot]
        column_block = left // LANES
        shift = left - column_block * LANES
        row_block = top // SUBLANES
        row_shift = top - row_block * SUBLANES
        rows = pl.ds(row_block, groups + 1)

        def columns(part):
            return pl.ds(pl.multiple_of((column_block + part) * LANES, LANES), LANES)

        patch = []
        back_shift = lax.rem(LANES - shift, LANES)
        back_row_shift = lax.rem(SUBLANES - row_shift, SUBLANES)
        keep = lane < LANES - shift
        keep_rows = sublane < SUBLANES - row_shift
        for comp in range(2):
            turned = [
                pltpu.roll(extended[comp, rows, :, columns(part)], back_shift, 2)
                for part in range(halves + 1)
            ]
            picked = []
            for part in range(halves):
                tall = pltpu.roll(
                    jnp.where(keep, turned[part], turned[part + 1]), back_row_shift, 1
                )
                picked.append(
                    jnp.where(keep_rows, tall[:groups], tall[1:]).reshape(size, LANES)
                )
            patch.append(
                jnp.concatenate(picked, axis=1).astype(jnp.bfloat16).astype(jnp.float32)
            )
        patch_real, patch_imag = patch
        probe_real, probe_imag = probe[0], probe[1]
        wave = jnp.concatenate(
            [
                probe_real * patch_real - probe_imag * patch_imag,
                probe_real * patch_imag + probe_imag * patch_real,
            ],
            axis=0,
        ).astype(jnp.bfloat16)
        near = dot(left_table[...], wave).astype(jnp.bfloat16)
        far = dot(jnp.concatenate([near[:size], near[size:]], axis=1), right_table[...])
        far_real, far_imag = far[:, :size], far[:, size:]
        power = far_real * far_real + far_imag * far_imag
        factor = 1.0 - amplitudes[slot].astype(jnp.float32) * lax.rsqrt(
            jnp.maximum(power, FLOOR * FLOOR)
        )
        misfit = jnp.concatenate([far_real * factor, far_imag * factor], axis=0).astype(
            jnp.bfloat16
        )
        back = dot(right_table[...], misfit).astype(jnp.bfloat16)
        update = dot(jnp.concatenate([back[:size], back[size:]], axis=1), left_table[...])
        update_real, update_imag = update[:, :size] * weight, update[:, size:] * weight
        terms = (
            patch_real * update_real + patch_imag * update_imag,
            patch_real * update_imag - patch_imag * update_real,
            (patch_real * patch_real + patch_imag * patch_imag) * weight,
        )
        for comp, term in enumerate(terms):
            for half in range(halves):
                sums[comp * halves + half] += term[:, half * LANES : (half + 1) * LANES]
        grads = (
            probe_real * update_real + probe_imag * update_imag,
            probe_real * update_imag - probe_imag * update_real,
        )
        moved = lane >= shift
        moved_rows = sublane >= row_shift
        for comp, grad in enumerate(grads):
            grad = grad.astype(jnp.bfloat16).astype(jnp.float32)
            turned = []
            for half in range(halves):
                tall = pltpu.roll(
                    grad[:, half * LANES : (half + 1) * LANES].reshape(groups, SUBLANES, LANES),
                    row_shift,
                    1,
                )
                tall = jnp.concatenate(
                    [
                        jnp.where(moved_rows[:1], tall[:1], 0.0),
                        jnp.where(moved_rows[1:], tall[1:], tall[:-1]),
                        jnp.where(moved_rows[:1], 0.0, tall[-1:]),
                    ],
                    axis=0,
                )
                turned.append(pltpu.roll(tall, shift, 2))
            nothing = jnp.zeros_like(turned[0])
            before = [nothing] + turned
            after = turned + [nothing]
            for part in range(halves + 1):
                gathered[comp, rows, :, columns(part)] += jnp.where(
                    moved, after[part], before[part]
                )

    count = live[0]

    def pair(index, carry):
        one_frame(2 * index, jnp.float32(1.0))
        one_frame(2 * index + 1, (2 * index + 1 < count).astype(jnp.float32))
        return carry

    lax.fori_loop(0, (count + 1) // 2, pair, 0)
    for _, target, rows, lanes in regions:
        target[...] = (
            gathered[:, grouped(rows), :, lanes].reshape(target.shape).astype(target.dtype)
        )


def frame_sums(block, rims, probe_field, amplitudes, positions, live, tables):
    size = probe_field.shape[-1]
    slots = amplitudes.shape[0]
    vmem = pl.BlockSpec(memory_space=pltpu.VMEM)
    smem = pl.BlockSpec(memory_space=pltpu.SMEM)
    planes, rows, columns = block.shape
    whole = (planes, (rows + size) // SUBLANES, SUBLANES, columns + size)
    return pl.pallas_call(
        frames_kernel,
        out_shape=(
            jax.ShapeDtypeStruct(block.shape, jnp.float32),
            *[jax.ShapeDtypeStruct(rim.shape, jnp.bfloat16) for rim in rims],
            jax.ShapeDtypeStruct((3 * size // LANES, size, LANES), jnp.float32),
        ),
        in_specs=[smem, smem] + [vmem] * 8,
        out_specs=(vmem,) * 5,
        scratch_shapes=[pltpu.VMEM(whole, jnp.float32), pltpu.VMEM(whole, jnp.float32)],
        compiler_params=pltpu.CompilerParams(vmem_limit_bytes=48 * 1024 * 1024),
        cost_estimate=pl.CostEstimate(
            flops=slots * 32 * size**3,
            bytes_accessed=12 * 1024 * 1024,
            transcendentals=slots * size * size,
        ),
        name="frames",
    )(positions, live, block, *rims, probe_field, amplitudes, *tables)


def remote(source, target, send, recv, device):
    return pltpu.make_async_remote_copy(
        src_ref=source,
        dst_ref=target,
        send_sem=send,
        recv_sem=recv,
        device_id=device,
        device_id_type=MESH,
    )


class Neighbours:

    def __init__(self, n_row, n_col):
        self.row, self.col = lax.axis_index("row"), lax.axis_index("col")
        self.above, self.under = self.row > 0, self.row < n_row - 1
        self.left, self.right = self.col > 0, self.col < n_col - 1

    def back(self):
        row, col = self.row, self.col
        return (
            (self.above, (row - 1, col)),
            (self.left, (row, col - 1)),
            (jnp.logical_and(self.above, self.left), (row - 1, col - 1)),
        )

    def ahead(self):
        row, col = self.row, self.col
        return (
            (self.under, (row + 1, col)),
            (self.right, (row, col + 1)),
            (jnp.logical_and(self.under, self.right), (row + 1, col + 1)),
        )


def greet(barrier, device):
    pl.semaphore_signal(barrier, inc=1, device_id=device, device_id_type=MESH)


def how_many(neighbours):
    return sum(there.astype(jnp.int32) for there, _ in neighbours)


def send_halos(near, narrow, rims, send, recv):
    _, height, _ = rims[0].shape
    _, _, width = rims[1].shape
    sources = (
        narrow.at[:, :height, :],
        narrow.at[:, :, :width],
        narrow.at[:, :height, :width],
    )
    sent = []
    for index, (there, device) in enumerate(near.back()):
        copy = remote(sources[index], rims[index], send.at[index], recv.at[index], device)
        pl.when(there)(copy.start)
        sent.append(copy)

    def finish():
        for copy, (there, _) in zip(sent, near.ahead()):
            pl.when(there)(copy.wait_recv)
        for copy, (there, _) in zip(sent, near.back()):
            pl.when(there)(copy.wait_send)

    return finish


def halo_kernel(n_row, n_col, block, below, beside, corner, narrow, send, recv):
    near = Neighbours(n_row, n_col)
    barrier = pltpu.get_barrier_semaphore()
    for there, device in near.back() + near.ahead():
        pl.when(there)(functools.partial(greet, barrier, device))
    narrow[...] = block[...].astype(jnp.bfloat16)
    pl.semaphore_wait(barrier, how_many(near.back() + near.ahead()))
    send_halos(near, narrow, (below, beside, corner), send, recv)()


def rim_shapes(block, size):
    planes, rows, columns = block.shape
    return tuple(
        jax.ShapeDtypeStruct(shape, jnp.bfloat16)
        for shape in ((planes, size, columns), (planes, rows, size), (planes, size, size))
    )


def first_halos(block, size):
    n_row, n_col = lax.axis_size("row"), lax.axis_size("col")
    hbm = pl.BlockSpec(memory_space=pl.ANY)
    dma = pltpu.SemaphoreType.DMA
    return pl.pallas_call(
        functools.partial(halo_kernel, n_row, n_col),
        out_shape=rim_shapes(block, size),
        in_specs=[pl.BlockSpec(memory_space=pltpu.VMEM)],
        out_specs=(hbm,) * 3,
        scratch_shapes=[pltpu.VMEM(block.shape, jnp.bfloat16), dma((3,)), dma((3,))],
        compiler_params=pltpu.CompilerParams(
            collective_id=0, has_side_effects=True, vmem_limit_bytes=32 * 1024 * 1024
        ),
        cost_estimate=pl.CostEstimate(
            flops=block.size, bytes_accessed=4 * 1024 * 1024, transcendentals=0
        ),
        name="first_halos",
    )(block)


def exchange_kernel(n_row, n_col, halos, *refs):
    block, own_grad, below_grad, beside_grad, corner_grad, sums, probe = refs[:7]
    refs = refs[7:]
    rims = ()
    new_block, out = refs[:2]
    refs = refs[2:]
    if halos:
        rims, refs = refs[:3], refs[3:]
    (
        got_below,
        got_beside,
        got_corner,
        narrow,
        wide,
        got_col,
        own_rows,
        got_row,
        piece,
        steps,
        joined,
        got_steps,
        grad_send,
        grad_recv,
        halo_send,
        halo_recv,
        col_send,
        col_recv,
        row_send,
        row_recv,
        back_row_send,
        back_row_recv,
        back_col_send,
        back_col_recv,
    ) = refs
    near = Neighbours(n_row, n_col)
    row, col = near.row, near.col
    planes, size, _ = sums.shape
    chunk = size // n_col
    part = chunk // n_row
    halves = planes // 3
    comps = 2 * halves

    def along_col(step):
        return (row, lax.rem(col + step, n_col))

    def along_row(step):
        return (lax.rem(row + step, n_row), col)

    barrier = pltpu.get_barrier_semaphore()
    for step in range(1, n_col):
        greet(barrier, along_col(step))
    for step in range(1, n_row):
        greet(barrier, along_row(step))
    corners = (near.back()[2], near.ahead()[2])
    for there, device in corners:
        pl.when(there)(functools.partial(greet, barrier, device))
    wide[...] = sums[...].astype(jnp.bfloat16)
    pl.semaphore_wait(barrier, n_col + n_row - 2 + how_many(corners))

    def started(source, target, send, recv, device):
        copy = remote(source, target, send, recv, device)
        copy.start()
        return copy

    def rows_of(index, length):
        return pl.ds(pl.multiple_of(index * length, length), length)

    first = []
    for step in range(1, n_col):
        their = lax.rem(col + step, n_col)
        first.append(
            started(
                wide.at[:, rows_of(their, chunk), :],
                got_col.at[step - 1],
                col_send.at[step - 1],
                col_recv.at[step - 1],
                along_col(step),
            )
        )
    grads = []
    pairs = ((below_grad, got_below), (beside_grad, got_beside), (corner_grad, got_corner))
    for index, (there, device) in enumerate(near.ahead()):
        source, target = pairs[index]
        copy = remote(source, target, grad_send.at[index], grad_recv.at[index], device)
        pl.when(there)(copy.start)
        grads.append(copy)
    step_size = ALPHA / (jnp.max(probe[0] * probe[0] + probe[1] * probe[1]) + 1e-06)
    new_block[...] = block[...] - step_size * own_grad[...]

    total = sums[:, rows_of(col, chunk), :]
    for step, copy in enumerate(first):
        copy.wait_recv()
        total = total + got_col[step].astype(jnp.float32)
    for index in range(n_row):
        own_rows[index] = total[:, index * part : (index + 1) * part, :]
    second = []
    for step in range(1, n_row):
        their = lax.rem(row + step, n_row)
        second.append(
            started(
                own_rows.at[their],
                got_row.at[step - 1],
                row_send.at[step - 1],
                row_recv.at[step - 1],
                along_row(step),
            )
        )

    for index, (there, _) in enumerate(near.back()):
        target = pairs[index][1]
        copy = grads[index]
        _, height, width = target.shape

        def add_rim():
            copy.wait_recv()
            new_block[:, :height, :width] -= step_size * target[...].astype(jnp.float32)

        pl.when(there)(add_rim)
    if halos:
        narrow[...] = new_block[...].astype(jnp.bfloat16)
        finish_halos = send_halos(near, narrow, rims, halo_send, halo_recv)

    total = own_rows[row]
    for step, copy in enumerate(second):
        copy.wait_recv()
        total = total + got_row[step]
    weight = total[2 * halves :] + 1.0
    piece[...] = jnp.concatenate(
        [total[:halves] / weight, total[halves : 2 * halves] / weight], axis=0
    )
    third = [
        started(
            piece,
            steps.at[row],
            back_row_send.at[step - 1],
            back_row_recv.at[step - 1],
            along_row(step),
        )
        for step in range(1, n_row)
    ]
    steps[row] = piece[...]
    for copy in third:
        copy.wait_recv()
    joined[...] = jnp.concatenate([steps[index] for index in range(n_row)], axis=1)
    fourth = [
        started(
            joined,
            got_steps.at[col],
            back_col_send.at[step - 1],
            back_col_recv.at[step - 1],
            along_col(step),
        )
        for step in range(1, n_col)
    ]
    got_steps[col] = joined[...]
    for copy in fourth:
        copy.wait_recv()
    for index in range(n_col):
        rows = slice(index * chunk, (index + 1) * chunk)
        for plane in range(comps):
            comp, half = divmod(plane, halves)
            lanes = slice(half * LANES, (half + 1) * LANES)
            out[comp, rows, lanes] = probe[comp, rows, lanes] - got_steps[index, plane]
    for copy in first + second + third + fourth:
        copy.wait_send()
    for copy, (there, _) in zip(grads, near.ahead()):
        pl.when(there)(copy.wait_send)
    if halos:
        finish_halos()


def exchange(block, own_grad, grad_rims, sums, probe_field, halos):
    n_row, n_col = lax.axis_size("row"), lax.axis_size("col")
    planes, size, _ = sums.shape
    chunk = size // n_col
    part = chunk // n_row
    comps = planes * 2 // 3
    vmem = pl.BlockSpec(memory_space=pltpu.VMEM)
    hbm = pl.BlockSpec(memory_space=pl.ANY)
    dma = pltpu.SemaphoreType.DMA
    shapes = rim_shapes(block, size)
    fresh = shapes if halos else ()
    new_block, new_probe, *rims = pl.pallas_call(
        functools.partial(exchange_kernel, n_row, n_col, halos),
        out_shape=(
            jax.ShapeDtypeStruct(block.shape, jnp.float32),
            jax.ShapeDtypeStruct(probe_field.shape, jnp.float32),
            *fresh,
        ),
        in_specs=[vmem, vmem, hbm, hbm, hbm, vmem, vmem],
        out_specs=(vmem, vmem) + (hbm,) * len(fresh),
        scratch_shapes=[
            *[pltpu.VMEM(shape.shape, shape.dtype) for shape in shapes],
            pltpu.VMEM(block.shape, jnp.bfloat16),
            pltpu.VMEM(sums.shape, jnp.bfloat16),
            pltpu.VMEM((n_col - 1, planes, chunk, LANES), jnp.bfloat16),
            pltpu.VMEM((n_row, planes, part, LANES), jnp.float32),
            pltpu.VMEM((n_row - 1, planes, part, LANES), jnp.float32),
            pltpu.VMEM((comps, part, LANES), jnp.float32),
            pltpu.VMEM((n_row, comps, part, LANES), jnp.float32),
            pltpu.VMEM((comps, chunk, LANES), jnp.float32),
            pltpu.VMEM((n_col, comps, chunk, LANES), jnp.float32),
            dma((3,)),
            dma((3,)),
            dma((3,)),
            dma((3,)),
            dma((n_col - 1,)),
            dma((n_col - 1,)),
            dma((n_row - 1,)),
            dma((n_row - 1,)),
            dma((n_row - 1,)),
            dma((n_row - 1,)),
            dma((n_col - 1,)),
            dma((n_col - 1,)),
        ],
        compiler_params=pltpu.CompilerParams(
            collective_id=1 if halos else 2,
            has_side_effects=True,
            vmem_limit_bytes=48 * 1024 * 1024,
        ),
        cost_estimate=pl.CostEstimate(
            flops=planes * size * LANES * 4, bytes_accessed=8 * 1024 * 1024, transcendentals=0
        ),
        name="exchange",
    )(block, own_grad, *grad_rims, sums, probe_field)
    return new_block, new_probe, tuple(rims)


def local(object_field, probe_field, amplitudes, positions, live_counts):
    frame_size = probe_field.shape[-1]
    tables = chirp_blocks(frame_size)
    rims = first_halos(object_field, frame_size)
    for iteration in range(ITERS):
        own_grad, *grad_rims, sums = frame_sums(
            object_field,
            rims,
            probe_field,
            amplitudes[iteration],
            positions[iteration],
            live_counts[iteration, 0],
            tables,
        )
        object_field, probe_field, rims = exchange(
            object_field, own_grad, grad_rims, sums, probe_field, iteration < ITERS - 1
        )
    return (object_field, probe_field)


def solution(mesh):
    placed = (
        P(None, "row", "col"),
        P(),
        P(None, ("row", "col"), None, None),
        P(None, None, ("row", "col")),
        P(None, "col", "row"),
    )
    return jax.shard_map(
        local, mesh=mesh, in_specs=placed, out_specs=(P(None, "row", "col"), P()), check_vma=False
    )
```

```python
import functools
import math

import jax
import jax.numpy as jnp
import ml_dtypes
import numpy as np
from jax import lax
from jax.experimental import pallas as pl
from jax.experimental.pallas import tpu as pltpu
from jax.sharding import PartitionSpec as P

ITERS = 2


FLOOR = 0.3
ALPHA = 0.5
LANES = 128
SUBLANES = 8
MESH = pl.DeviceIdType.MESH


def chirp_blocks(frame_size):
    offset = np.arange(frame_size, dtype=np.int32)
    differ = offset[:, None] - offset[None, :]
    phase = np.pi * (differ * differ % (2 * frame_size)).astype(np.float64) / frame_size
    scale = 1.0 / math.sqrt(frame_size)
    real, imag = (np.cos(phase) * scale, np.sin(phase) * scale)
    forward = np.block([[real, -imag], [imag, real]]).astype(ml_dtypes.bfloat16)
    return jnp.asarray(forward), jnp.asarray(forward.T.copy())


def local_copy(source, target, semaphore):
    copy = pltpu.make_async_copy(source, target, semaphore)
    copy.start()
    return copy


def frames_kernel(
    iteration,
    positions,
    live,
    block,
    below,
    beside,
    corner,
    probe_hbm,
    amplitudes_hbm,
    left_hbm,
    right_hbm,
    own_grad,
    below_grad,
    beside_grad,
    corner_grad,
    sums,
    extended,
    gathered,
    below_held,
    beside_held,
    corner_held,
    probe,
    amplitudes,
    left_table,
    right_table,
    semaphores,
):
    size = probe.shape[-1]
    halves = size // LANES
    _, row_groups, _, block_columns = block.shape
    inner = (slice(None), slice(0, row_groups), slice(None), slice(0, block_columns))
    regions = (
        (below_held, below_grad, slice(row_groups, None), slice(0, block_columns)),
        (beside_held, beside_grad, slice(0, row_groups), slice(block_columns, None)),
        (corner_held, corner_grad, slice(row_groups, None), slice(block_columns, None)),
    )
    moves = (
        (below, below_held),
        (beside, beside_held),
        (corner, corner_held),
        (block, extended.at[inner]),
        (probe_hbm, probe),
        (left_hbm, left_table),
        (amplitudes_hbm.at[iteration], amplitudes),
        (right_hbm, right_table),
    )
    copies = [
        local_copy(source, target, semaphores.at[index])
        for index, (source, target) in enumerate(moves)
    ]
    gathered[...] = jnp.zeros_like(gathered)
    sums[...] = jnp.zeros_like(sums)
    for copy, (source, _, groups, lanes) in zip(copies, regions):
        copy.wait()
        planes, tall, width = source.shape
        extended[:, groups, :, lanes] = (
            source[...].astype(jnp.float32).reshape(planes, tall // SUBLANES, SUBLANES, width)
        )
    for copy in copies[len(regions) :]:
        copy.wait()
    groups = size // SUBLANES
    lane = lax.broadcasted_iota(jnp.int32, (groups + 1, SUBLANES, LANES), 2)
    sublane = lax.broadcasted_iota(jnp.int32, (groups, SUBLANES, LANES), 1)

    def dot(a, b):
        return jnp.dot(a, b, preferred_element_type=jnp.float32)

    def one_frame(slot, weight):
        top = positions[iteration, 0, slot]
        left = positions[iteration, 1, slot]
        column_block = left // LANES
        shift = left - column_block * LANES
        row_block = top // SUBLANES
        row_shift = top - row_block * SUBLANES
        rows = pl.ds(row_block, groups + 1)

        def columns(part):
            return pl.ds(pl.multiple_of((column_block + part) * LANES, LANES), LANES)

        patch = []
        back_shift = lax.rem(LANES - shift, LANES)
        back_row_shift = lax.rem(SUBLANES - row_shift, SUBLANES)
        keep = lane < LANES - shift
        keep_rows = sublane < SUBLANES - row_shift
        for comp in range(2):
            turned = [
                pltpu.roll(extended[comp, rows, :, columns(part)], back_shift, 2)
                for part in range(halves + 1)
            ]
            picked = []
            for part in range(halves):
                tall = pltpu.roll(
                    jnp.where(keep, turned[part], turned[part + 1]), back_row_shift, 1
                )
                picked.append(
                    jnp.where(keep_rows, tall[:groups], tall[1:]).reshape(size, LANES)
                )
            patch.append(
                jnp.concatenate(picked, axis=1).astype(jnp.bfloat16).astype(jnp.float32)
            )
        patch_real, patch_imag = patch
        probe_real, probe_imag = probe[0], probe[1]
        wave = jnp.concatenate(
            [
                probe_real * patch_real - probe_imag * patch_imag,
                probe_real * patch_imag + probe_imag * patch_real,
            ],
            axis=0,
        ).astype(jnp.bfloat16)
        near = dot(left_table[...], wave).astype(jnp.bfloat16)
        far = dot(jnp.concatenate([near[:size], near[size:]], axis=1), right_table[...])
        far_real, far_imag = far[:, :size], far[:, size:]
        power = far_real * far_real + far_imag * far_imag
        factor = 1.0 - amplitudes[slot].astype(jnp.float32) * lax.rsqrt(
            jnp.maximum(power, FLOOR * FLOOR)
        )
        misfit = jnp.concatenate([far_real * factor, far_imag * factor], axis=0).astype(
            jnp.bfloat16
        )
        back = dot(right_table[...], misfit).astype(jnp.bfloat16)
        update = dot(jnp.concatenate([back[:size], back[size:]], axis=1), left_table[...])
        update_real, update_imag = update[:, :size] * weight, update[:, size:] * weight
        terms = (
            patch_real * update_real + patch_imag * update_imag,
            patch_real * update_imag - patch_imag * update_real,
            (patch_real * patch_real + patch_imag * patch_imag) * weight,
        )
        for comp, term in enumerate(terms):
            for half in range(halves):
                sums[comp * halves + half] += term[:, half * LANES : (half + 1) * LANES]
        grads = (
            probe_real * update_real + probe_imag * update_imag,
            probe_real * update_imag - probe_imag * update_real,
        )
        moved = lane >= shift
        moved_rows = sublane >= row_shift
        for comp, grad in enumerate(grads):
            grad = grad.astype(jnp.bfloat16).astype(jnp.float32)
            turned = []
            for half in range(halves):
                tall = pltpu.roll(
                    grad[:, half * LANES : (half + 1) * LANES].reshape(groups, SUBLANES, LANES),
                    row_shift,
                    1,
                )
                tall = jnp.concatenate(
                    [
                        jnp.where(moved_rows[:1], tall[:1], 0.0),
                        jnp.where(moved_rows[1:], tall[1:], tall[:-1]),
                        jnp.where(moved_rows[:1], 0.0, tall[-1:]),
                    ],
                    axis=0,
                )
                turned.append(pltpu.roll(tall, shift, 2))
            nothing = jnp.zeros_like(turned[0])
            before = [nothing] + turned
            after = turned + [nothing]
            for part in range(halves + 1):
                gathered[comp, rows, :, columns(part)] += jnp.where(
                    moved, after[part], before[part]
                )

    count = live[iteration, 0, 0]

    def pair(index, carry):
        one_frame(2 * index, jnp.float32(1.0))
        one_frame(2 * index + 1, (2 * index + 1 < count).astype(jnp.float32))
        return carry

    lax.fori_loop(0, (count + 1) // 2, pair, 0)
    leaving = local_copy(gathered.at[inner], own_grad, semaphores.at[0])
    for _, target, groups, lanes in regions:
        target[...] = gathered[:, groups, :, lanes].reshape(target.shape).astype(target.dtype)
    leaving.wait()


def frame_sums(block, rims, probe_field, amplitudes, positions, live, tables, iteration):
    size = probe_field.shape[-1]
    slots = amplitudes.shape[1]
    vmem = pl.BlockSpec(memory_space=pltpu.VMEM)
    smem = pl.BlockSpec(memory_space=pltpu.SMEM)
    hbm = pl.BlockSpec(memory_space=pl.ANY)
    planes, row_groups, _, columns = block.shape
    whole = (planes, row_groups + size // SUBLANES, SUBLANES, columns + size)
    held = [*rims, probe_field, amplitudes[0], *tables]
    return pl.pallas_call(
        functools.partial(frames_kernel, iteration),
        out_shape=(
            jax.ShapeDtypeStruct(block.shape, jnp.float32),
            *[jax.ShapeDtypeStruct(rim.shape, jnp.bfloat16) for rim in rims],
            jax.ShapeDtypeStruct((3 * size // LANES, size, LANES), jnp.float32),
        ),
        in_specs=[smem, smem] + [hbm] * 8,
        out_specs=(hbm,) + (vmem,) * 4,
        scratch_shapes=[
            pltpu.VMEM(whole, jnp.float32),
            pltpu.VMEM(whole, jnp.float32),
            *[pltpu.VMEM(value.shape, value.dtype) for value in held],
            pltpu.SemaphoreType.DMA((8,)),
        ],
        compiler_params=pltpu.CompilerParams(vmem_limit_bytes=48 * 1024 * 1024),
        cost_estimate=pl.CostEstimate(
            flops=slots * 32 * size**3,
            bytes_accessed=12 * 1024 * 1024,
            transcendentals=slots * size * size,
        ),
        name="frames",
    )(positions, live, block, *rims, probe_field, amplitudes, *tables)


def remote(source, target, send, recv, device):
    return pltpu.make_async_remote_copy(
        src_ref=source,
        dst_ref=target,
        send_sem=send,
        recv_sem=recv,
        device_id=device,
        device_id_type=MESH,
    )


class Neighbours:

    def __init__(self, n_row, n_col):
        self.row, self.col = lax.axis_index("row"), lax.axis_index("col")
        self.above, self.under = self.row > 0, self.row < n_row - 1
        self.left, self.right = self.col > 0, self.col < n_col - 1

    def back(self):
        row, col = self.row, self.col
        return (
            (self.above, (row - 1, col)),
            (self.left, (row, col - 1)),
            (jnp.logical_and(self.above, self.left), (row - 1, col - 1)),
        )

    def ahead(self):
        row, col = self.row, self.col
        return (
            (self.under, (row + 1, col)),
            (self.right, (row, col + 1)),
            (jnp.logical_and(self.under, self.right), (row + 1, col + 1)),
        )


def greet(barrier, device):
    pl.semaphore_signal(barrier, inc=1, device_id=device, device_id_type=MESH)


def how_many(neighbours):
    return sum(there.astype(jnp.int32) for there, _ in neighbours)


def send_halos(near, narrow, rims, send, recv):
    _, height, _ = rims[0].shape
    _, _, width = rims[1].shape
    sources = (
        narrow.at[:, :height, :],
        narrow.at[:, :, :width],
        narrow.at[:, :height, :width],
    )
    sent = []
    for index, (there, device) in enumerate(near.back()):
        copy = remote(sources[index], rims[index], send.at[index], recv.at[index], device)
        pl.when(there)(copy.start)
        sent.append(copy)

    def finish():
        for copy, (there, _) in zip(sent, near.ahead()):
            pl.when(there)(copy.wait_recv)
        for copy, (there, _) in zip(sent, near.back()):
            pl.when(there)(copy.wait_send)

    return finish


def halo_kernel(n_row, n_col, block, below, beside, corner, narrow, send, recv):
    near = Neighbours(n_row, n_col)
    barrier = pltpu.get_barrier_semaphore()
    for there, device in near.back() + near.ahead():
        pl.when(there)(functools.partial(greet, barrier, device))
    narrow[...] = block[...].astype(jnp.bfloat16)
    pl.semaphore_wait(barrier, how_many(near.back() + near.ahead()))
    send_halos(near, narrow, (below, beside, corner), send, recv)()


def rim_shapes(block, size):
    planes, rows, columns = block.shape
    return tuple(
        jax.ShapeDtypeStruct(shape, jnp.bfloat16)
        for shape in ((planes, size, columns), (planes, rows, size), (planes, size, size))
    )


def first_halos(block, size):
    n_row, n_col = lax.axis_size("row"), lax.axis_size("col")
    hbm = pl.BlockSpec(memory_space=pl.ANY)
    dma = pltpu.SemaphoreType.DMA
    return pl.pallas_call(
        functools.partial(halo_kernel, n_row, n_col),
        out_shape=rim_shapes(block, size),
        in_specs=[pl.BlockSpec(memory_space=pltpu.VMEM)],
        out_specs=(hbm,) * 3,
        scratch_shapes=[pltpu.VMEM(block.shape, jnp.bfloat16), dma((3,)), dma((3,))],
        compiler_params=pltpu.CompilerParams(
            collective_id=0, has_side_effects=True, vmem_limit_bytes=32 * 1024 * 1024
        ),
        cost_estimate=pl.CostEstimate(
            flops=block.size, bytes_accessed=4 * 1024 * 1024, transcendentals=0
        ),
        name="first_halos",
    )(block)


def exchange_kernel(n_row, n_col, halos, *refs):
    block_hbm, own_grad_hbm, below_grad, beside_grad, corner_grad, sums_hbm, probe_hbm = refs[:7]
    refs = refs[7:]
    rims = ()
    new_block, out = refs[:2]
    refs = refs[2:]
    if halos:
        rims, refs = refs[:3], refs[3:]
    (
        block,
        own_grad,
        sums,
        probe,
        load,
        got_below,
        got_beside,
        got_corner,
        narrow,
        wide,
        got_col,
        own_rows,
        got_row,
        piece,
        steps,
        joined,
        got_steps,
        grad_send,
        grad_recv,
        halo_send,
        halo_recv,
        col_send,
        col_recv,
        row_send,
        row_recv,
        back_row_send,
        back_row_recv,
        back_col_send,
        back_col_recv,
        core_send,
        core_recv,
    ) = refs
    loads = [
        local_copy(source, target, load.at[index])
        for index, (source, target) in enumerate(
            ((sums_hbm, sums), (probe_hbm, probe), (block_hbm, block), (own_grad_hbm, own_grad))
        )
    ]
    near = Neighbours(n_row, n_col)
    row, col = near.row, near.col
    planes, size, _ = sums.shape
    chunk = size // n_col
    part = chunk // n_row
    halves = planes // 3
    comps = 2 * halves

    def along_col(step):
        return (row, lax.rem(col + step, n_col))

    def along_row(step):
        return (lax.rem(row + step, n_row), col)

    barrier = pltpu.get_barrier_semaphore()
    for step in range(1, n_col):
        greet(barrier, along_col(step))
    for step in range(1, n_row):
        greet(barrier, along_row(step))
    corners = (near.back()[2], near.ahead()[2])
    for there, device in corners:
        pl.when(there)(functools.partial(greet, barrier, device))
    loads[0].wait()
    wide[...] = sums[...].astype(jnp.bfloat16)
    pl.semaphore_wait(barrier, n_col + n_row - 2 + how_many(corners))

    def started(source, target, send, recv, device):
        copy = remote(source, target, send, recv, device)
        copy.start()
        return copy

    def rows_of(index, length):
        return pl.ds(pl.multiple_of(index * length, length), length)

    first = []
    for step in range(1, n_col):
        their = lax.rem(col + step, n_col)
        first.append(
            started(
                wide.at[:, rows_of(their, chunk), :],
                got_col.at[step - 1],
                col_send.at[step - 1],
                col_recv.at[step - 1],
                along_col(step),
            )
        )
    grads = []
    pairs = ((below_grad, got_below), (beside_grad, got_beside), (corner_grad, got_corner))
    for index, (there, device) in enumerate(near.ahead()):
        source, target = pairs[index]
        copy = remote(source, target, grad_send.at[index], grad_recv.at[index], device)
        pl.when(there)(copy.start)
        grads.append(copy)
    for copy in loads[1:]:
        copy.wait()
    step_size = ALPHA / (jnp.max(probe[0] * probe[0] + probe[1] * probe[1]) + 1e-06)
    new_block[...] = block[...] - step_size * own_grad[...]

    total = sums[:, rows_of(col, chunk), :]
    for step, copy in enumerate(first):
        copy.wait_recv()
        total = total + got_col[step].astype(jnp.float32)
    for index in range(n_row):
        own_rows[index] = total[:, index * part : (index + 1) * part, :]
    second = []
    for step in range(1, n_row):
        their = lax.rem(row + step, n_row)
        second.append(
            started(
                own_rows.at[their],
                got_row.at[step - 1],
                row_send.at[step - 1],
                row_recv.at[step - 1],
                along_row(step),
            )
        )

    total = own_rows[row]
    for step, copy in enumerate(second):
        copy.wait_recv()
        total = total + got_row[step]
    weight = total[2 * halves :] + 1.0
    piece[...] = jnp.concatenate(
        [total[:halves] / weight, total[halves : 2 * halves] / weight], axis=0
    )
    third = [
        started(
            piece,
            steps.at[row],
            back_row_send.at[step - 1],
            back_row_recv.at[step - 1],
            along_row(step),
        )
        for step in range(1, n_row)
    ]
    steps[row] = piece[...]
    for copy in third:
        copy.wait_recv()
    joined[...] = jnp.concatenate([steps[index] for index in range(n_row)], axis=1)
    got_steps[col] = joined[...]
    count = n_col // 2
    place, core = col // 2, lax.rem(col, 2)
    other = (row, col + 1 - 2 * core)
    across = [
        started(
            joined,
            got_steps.at[col],
            back_col_send.at[step - 1],
            back_col_recv.at[step - 1],
            (row, lax.rem(place + step, count) * 2 + core),
        )
        for step in range(1, count)
    ]
    over = [started(joined, got_steps.at[col], core_send.at[0], core_recv.at[0], other)]

    for index, (there, _) in enumerate(near.back()):
        target = pairs[index][1]
        copy = grads[index]
        _, height, width = target.shape

        def add_rim():
            copy.wait_recv()
            new_block[:, :height, :width] -= step_size * target[...].astype(jnp.float32)

        pl.when(there)(add_rim)
    if halos:
        narrow[...] = new_block[...].astype(jnp.bfloat16)
        finish_halos = send_halos(near, narrow, rims, halo_send, halo_recv)


    for step in range(1, count):
        across[step - 1].wait_recv()
        slot = got_steps.at[lax.rem(place + count - step, count) * 2 + core]
        over.append(started(slot, slot, core_send.at[step], core_recv.at[step], other))
    for copy in over:
        copy.wait_recv()
    for index in range(n_col):
        rows = slice(index * chunk, (index + 1) * chunk)
        for plane in range(comps):
            comp, half = divmod(plane, halves)
            lanes = slice(half * LANES, (half + 1) * LANES)
            out[comp, rows, lanes] = probe[comp, rows, lanes] - got_steps[index, plane]
    for copy in first + second + third + across + over:
        copy.wait_send()
    for copy, (there, _) in zip(grads, near.ahead()):
        pl.when(there)(copy.wait_send)
    if halos:
        finish_halos()


def exchange(block, own_grad, grad_rims, sums, probe_field, halos):
    n_row, n_col = lax.axis_size("row"), lax.axis_size("col")
    planes, size, _ = sums.shape
    chunk = size // n_col
    part = chunk // n_row
    comps = planes * 2 // 3
    vmem = pl.BlockSpec(memory_space=pltpu.VMEM)
    hbm = pl.BlockSpec(memory_space=pl.ANY)
    dma = pltpu.SemaphoreType.DMA
    shapes = rim_shapes(block, size)
    fresh = shapes if halos else ()
    new_block, new_probe, *rims = pl.pallas_call(
        functools.partial(exchange_kernel, n_row, n_col, halos),
        out_shape=(
            jax.ShapeDtypeStruct(block.shape, jnp.float32),
            jax.ShapeDtypeStruct(probe_field.shape, jnp.float32),
            *fresh,
        ),
        in_specs=[hbm] * 7,
        out_specs=(vmem, vmem) + (hbm,) * len(fresh),
        scratch_shapes=[
            *[pltpu.VMEM(value.shape, jnp.float32) for value in (block, own_grad, sums, probe_field)],
            dma((4,)),
            *[pltpu.VMEM(shape.shape, shape.dtype) for shape in shapes],
            pltpu.VMEM(block.shape, jnp.bfloat16),
            pltpu.VMEM(sums.shape, jnp.bfloat16),
            pltpu.VMEM((n_col - 1, planes, chunk, LANES), jnp.bfloat16),
            pltpu.VMEM((n_row, planes, part, LANES), jnp.float32),
            pltpu.VMEM((n_row - 1, planes, part, LANES), jnp.float32),
            pltpu.VMEM((comps, part, LANES), jnp.float32),
            pltpu.VMEM((n_row, comps, part, LANES), jnp.float32),
            pltpu.VMEM((comps, chunk, LANES), jnp.float32),
            pltpu.VMEM((n_col, comps, chunk, LANES), jnp.float32),
            dma((3,)),
            dma((3,)),
            dma((3,)),
            dma((3,)),
            dma((n_col - 1,)),
            dma((n_col - 1,)),
            dma((n_row - 1,)),
            dma((n_row - 1,)),
            dma((n_row - 1,)),
            dma((n_row - 1,)),
            dma((n_col // 2,)),
            dma((n_col // 2,)),
            dma((n_col // 2,)),
            dma((n_col // 2,)),
        ],
        compiler_params=pltpu.CompilerParams(
            collective_id=1 if halos else 2,
            has_side_effects=True,
            vmem_limit_bytes=48 * 1024 * 1024,
        ),
        cost_estimate=pl.CostEstimate(
            flops=planes * size * LANES * 4, bytes_accessed=8 * 1024 * 1024, transcendentals=0
        ),
        name="exchange",
    )(block, own_grad, *grad_rims, sums, probe_field)
    return new_block, new_probe, tuple(rims)


def local(object_field, probe_field, amplitudes, positions, live_counts):
    frame_size = probe_field.shape[-1]
    tables = chirp_blocks(frame_size)
    rims = first_halos(object_field, frame_size)
    for iteration in range(ITERS):
        planes, rows, columns = object_field.shape
        own_grad, *grad_rims, sums = frame_sums(
            object_field.reshape(planes, rows // SUBLANES, SUBLANES, columns),
            rims,
            probe_field,
            amplitudes,
            positions,
            live_counts,
            tables,
            iteration,
        )
        own_grad = own_grad.reshape(object_field.shape)
        object_field, probe_field, rims = exchange(
            object_field, own_grad, grad_rims, sums, probe_field, iteration < ITERS - 1
        )
    return (object_field, probe_field)


def solution(mesh):
    placed = (
        P(None, "row", "col"),
        P(),
        P(None, ("row", "col"), None, None),
        P(None, None, ("row", "col")),
        P(None, "col", "row"),
    )
    return jax.shard_map(
        local, mesh=mesh, in_specs=placed, out_specs=(P(None, "row", "col"), P()), check_vma=False
    )
```

```python
import functools
import math

import jax
import jax.numpy as jnp
import ml_dtypes
import numpy as np
from jax import lax
from jax.experimental import pallas as pl
from jax.experimental.pallas import tpu as pltpu
from jax.sharding import PartitionSpec as P

ITERS = 2


FLOOR = 0.3
ALPHA = 0.5
LANES = 128
SUBLANES = 8
MESH = pl.DeviceIdType.MESH


def chirp_blocks(frame_size):
    offset = np.arange(frame_size, dtype=np.int32)
    differ = offset[:, None] - offset[None, :]
    phase = np.pi * (differ * differ % (2 * frame_size)).astype(np.float64) / frame_size
    scale = 1.0 / math.sqrt(frame_size)
    real, imag = (np.cos(phase) * scale, np.sin(phase) * scale)
    forward = np.block([[real, -imag], [imag, real]]).astype(ml_dtypes.bfloat16)
    return jnp.asarray(forward), jnp.asarray(forward.T.copy())


def local_copy(source, target, semaphore):
    copy = pltpu.make_async_copy(source, target, semaphore)
    copy.start()
    return copy


def frames_kernel(
    iteration,
    positions,
    live,
    block,
    below,
    beside,
    corner,
    probe_hbm,
    amplitudes_hbm,
    left_hbm,
    right_hbm,
    own_grad,
    below_grad,
    beside_grad,
    corner_grad,
    sums,
    extended,
    gathered,
    below_held,
    beside_held,
    corner_held,
    probe,
    amplitudes,
    left_table,
    right_table,
    semaphores,
):
    size = probe.shape[-1]
    halves = size // LANES
    _, row_groups, _, block_columns = block.shape
    inner = (slice(None), slice(0, row_groups), slice(None), slice(0, block_columns))
    regions = (
        (below_held, below_grad, slice(row_groups, None), slice(0, block_columns)),
        (beside_held, beside_grad, slice(0, row_groups), slice(block_columns, None)),
        (corner_held, corner_grad, slice(row_groups, None), slice(block_columns, None)),
    )
    moves = (
        (below, below_held),
        (beside, beside_held),
        (corner, corner_held),
        (block, extended.at[inner]),
        (probe_hbm, probe),
        (left_hbm, left_table),
        (amplitudes_hbm.at[iteration], amplitudes),
        (right_hbm, right_table),
    )
    copies = [
        local_copy(source, target, semaphores.at[index])
        for index, (source, target) in enumerate(moves)
    ]
    gathered[...] = jnp.zeros_like(gathered)
    sums[...] = jnp.zeros_like(sums)
    for copy, (source, _, groups, lanes) in zip(copies, regions):
        copy.wait()
        planes, tall, width = source.shape
        extended[:, groups, :, lanes] = (
            source[...].astype(jnp.float32).reshape(planes, tall // SUBLANES, SUBLANES, width)
        )
    for copy in copies[len(regions) :]:
        copy.wait()
    groups = size // SUBLANES
    lane = lax.broadcasted_iota(jnp.int32, (groups + 1, SUBLANES, LANES), 2)
    sublane = lax.broadcasted_iota(jnp.int32, (groups, SUBLANES, LANES), 1)

    def dot(a, b):
        return jnp.dot(a, b, preferred_element_type=jnp.float32)

    def one_frame(slot, weight=None):
        top = positions[iteration, 0, slot]
        left = positions[iteration, 1, slot]
        column_block = left // LANES
        shift = left - column_block * LANES
        row_block = top // SUBLANES
        row_shift = top - row_block * SUBLANES
        rows = pl.ds(row_block, groups + 1)

        def columns(part):
            return pl.ds(pl.multiple_of((column_block + part) * LANES, LANES), LANES)

        patch = []
        back_shift = lax.rem(LANES - shift, LANES)
        back_row_shift = lax.rem(SUBLANES - row_shift, SUBLANES)
        keep = lane < LANES - shift
        keep_rows = sublane < SUBLANES - row_shift
        for comp in range(2):
            turned = [
                pltpu.roll(extended[comp, rows, :, columns(part)], back_shift, 2)
                for part in range(halves + 1)
            ]
            picked = []
            for part in range(halves):
                tall = pltpu.roll(
                    jnp.where(keep, turned[part], turned[part + 1]), back_row_shift, 1
                )
                picked.append(
                    jnp.where(keep_rows, tall[:groups], tall[1:]).reshape(size, LANES)
                )
            patch.append(
                jnp.concatenate(picked, axis=1).astype(jnp.bfloat16).astype(jnp.float32)
            )
        patch_real, patch_imag = patch
        probe_real, probe_imag = probe[0], probe[1]
        wave = jnp.concatenate(
            [
                probe_real * patch_real - probe_imag * patch_imag,
                probe_real * patch_imag + probe_imag * patch_real,
            ],
            axis=0,
        ).astype(jnp.bfloat16)
        yield
        near = dot(left_table[...], wave).astype(jnp.bfloat16)
        yield
        far = dot(jnp.concatenate([near[:size], near[size:]], axis=1), right_table[...])
        yield
        far_real, far_imag = far[:, :size], far[:, size:]
        power = far_real * far_real + far_imag * far_imag
        factor = 1.0 - amplitudes[slot].astype(jnp.float32) * lax.rsqrt(
            jnp.maximum(power, FLOOR * FLOOR)
        )
        misfit = jnp.concatenate([far_real * factor, far_imag * factor], axis=0).astype(
            jnp.bfloat16
        )
        yield
        back = dot(right_table[...], misfit).astype(jnp.bfloat16)
        yield
        update = dot(jnp.concatenate([back[:size], back[size:]], axis=1), left_table[...])
        yield
        update_real, update_imag = update[:, :size], update[:, size:]
        density = patch_real * patch_real + patch_imag * patch_imag
        if weight is not None:
            update_real, update_imag = update_real * weight, update_imag * weight
            density = density * weight
        terms = (
            patch_real * update_real + patch_imag * update_imag,
            patch_real * update_imag - patch_imag * update_real,
            density,
        )
        for comp, term in enumerate(terms):
            for half in range(halves):
                sums[comp * halves + half] += term[:, half * LANES : (half + 1) * LANES]
        grads = (
            probe_real * update_real + probe_imag * update_imag,
            probe_real * update_imag - probe_imag * update_real,
        )
        moved = lane >= shift
        moved_rows = sublane >= row_shift
        for comp, grad in enumerate(grads):
            grad = grad.astype(jnp.bfloat16).astype(jnp.float32)
            turned = []
            for half in range(halves):
                tall = pltpu.roll(
                    grad[:, half * LANES : (half + 1) * LANES].reshape(groups, SUBLANES, LANES),
                    row_shift,
                    1,
                )
                tall = jnp.concatenate(
                    [
                        jnp.where(moved_rows[:1], tall[:1], 0.0),
                        jnp.where(moved_rows[1:], tall[1:], tall[:-1]),
                        jnp.where(moved_rows[:1], 0.0, tall[-1:]),
                    ],
                    axis=0,
                )
                turned.append(pltpu.roll(tall, shift, 2))
            nothing = jnp.zeros_like(turned[0])
            before = [nothing] + turned
            after = turned + [nothing]
            for part in range(halves + 1):
                gathered[comp, rows, :, columns(part)] += jnp.where(
                    moved, after[part], before[part]
                )

    count = live[iteration, 0, 0]

    def pair(index, carry):
        second_weight = (2 * index + 1 < count).astype(jnp.float32)
        leading = one_frame(2 * index)
        lagging = one_frame(2 * index + 1, second_weight)
        next(leading)
        for running in (leading, lagging) * 7:
            next(running, None)
        return carry

    lax.fori_loop(0, (count + 1) // 2, pair, 0)
    leaving = local_copy(gathered.at[inner], own_grad, semaphores.at[0])
    for _, target, groups, lanes in regions:
        target[...] = gathered[:, groups, :, lanes].reshape(target.shape).astype(target.dtype)
    leaving.wait()


def frame_sums(block, rims, probe_field, amplitudes, positions, live, tables, iteration):
    size = probe_field.shape[-1]
    slots = amplitudes.shape[1]
    vmem = pl.BlockSpec(memory_space=pltpu.VMEM)
    smem = pl.BlockSpec(memory_space=pltpu.SMEM)
    hbm = pl.BlockSpec(memory_space=pl.ANY)
    planes, row_groups, _, columns = block.shape
    whole = (planes, row_groups + size // SUBLANES, SUBLANES, columns + size)
    held = [*rims, probe_field, amplitudes[0], *tables]
    return pl.pallas_call(
        functools.partial(frames_kernel, iteration),
        out_shape=(
            jax.ShapeDtypeStruct(block.shape, jnp.float32),
            *[jax.ShapeDtypeStruct(rim.shape, jnp.bfloat16) for rim in rims],
            jax.ShapeDtypeStruct((3 * size // LANES, size, LANES), jnp.float32),
        ),
        in_specs=[smem, smem] + [hbm] * 8,
        out_specs=(hbm,) + (vmem,) * 4,
        scratch_shapes=[
            pltpu.VMEM(whole, jnp.float32),
            pltpu.VMEM(whole, jnp.float32),
            *[pltpu.VMEM(value.shape, value.dtype) for value in held],
            pltpu.SemaphoreType.DMA((8,)),
        ],
        compiler_params=pltpu.CompilerParams(vmem_limit_bytes=48 * 1024 * 1024),
        cost_estimate=pl.CostEstimate(
            flops=slots * 32 * size**3,
            bytes_accessed=12 * 1024 * 1024,
            transcendentals=slots * size * size,
        ),
        name="frames",
    )(positions, live, block, *rims, probe_field, amplitudes, *tables)


def remote(source, target, send, recv, device):
    return pltpu.make_async_remote_copy(
        src_ref=source,
        dst_ref=target,
        send_sem=send,
        recv_sem=recv,
        device_id=device,
        device_id_type=MESH,
    )


class Neighbours:

    def __init__(self, n_row, n_col):
        self.row, self.col = lax.axis_index("row"), lax.axis_index("col")
        self.above, self.under = self.row > 0, self.row < n_row - 1
        self.left, self.right = self.col > 0, self.col < n_col - 1

    def back(self):
        row, col = self.row, self.col
        return (
            (self.above, (row - 1, col)),
            (self.left, (row, col - 1)),
        )

    def ahead(self):
        row, col = self.row, self.col
        return (
            (self.under, (row + 1, col)),
            (self.right, (row, col + 1)),
        )


def greet(barrier, device):
    pl.semaphore_signal(barrier, inc=1, device_id=device, device_id_type=MESH)


def how_many(neighbours):
    return sum(there.astype(jnp.int32) for there, _ in neighbours)


def send_halos(near, narrow, rims, send, recv):
    below, beside, corner = rims
    _, height, size = corner.shape
    (above, up), (left, aside) = near.back()
    (under, _), (right, _) = near.ahead()
    first, rest = slice(0, size), slice(size, None)
    pieces = (
        (narrow.at[:, :height, first], below.at[:, :, first], up),
        (narrow.at[:, :height, rest], below.at[:, :, rest], up),
        (narrow.at[:, :, first], beside, aside),
        (below.at[:, :, first], corner, aside),
    )
    sent = [
        remote(source, target, send.at[index], recv.at[index], device)
        for index, (source, target, device) in enumerate(pieces)
    ]
    relays = jnp.logical_and(under, left)
    relayed = jnp.logical_and(under, right)
    for copy, there in zip(sent, (above, above, left)):
        pl.when(there)(copy.start)

    def relay():
        pl.when(under)(sent[0].wait_recv)
        pl.when(relays)(sent[3].start)

    def finish():
        for copy, there in zip(sent[1:], (under, right, relayed)):
            pl.when(there)(copy.wait_recv)
        for copy, there in zip(sent, (above, above, left, relays)):
            pl.when(there)(copy.wait_send)

    return relay, finish


def halo_kernel(n_row, n_col, block, below, beside, corner, narrow, send, recv):
    near = Neighbours(n_row, n_col)
    barrier = pltpu.get_barrier_semaphore()
    for there, device in near.back() + near.ahead():
        pl.when(there)(functools.partial(greet, barrier, device))
    narrow[...] = block[...].astype(jnp.bfloat16)
    pl.semaphore_wait(barrier, how_many(near.back() + near.ahead()))
    relay, finish = send_halos(near, narrow, (below, beside, corner), send, recv)
    relay()
    finish()


def rim_shapes(block, size):
    planes, rows, columns = block.shape
    return tuple(
        jax.ShapeDtypeStruct(shape, jnp.bfloat16)
        for shape in ((planes, size, columns), (planes, rows, size), (planes, size, size))
    )


def first_halos(block, size):
    n_row, n_col = lax.axis_size("row"), lax.axis_size("col")
    hbm = pl.BlockSpec(memory_space=pl.ANY)
    dma = pltpu.SemaphoreType.DMA
    return pl.pallas_call(
        functools.partial(halo_kernel, n_row, n_col),
        out_shape=rim_shapes(block, size),
        in_specs=[pl.BlockSpec(memory_space=pltpu.VMEM)],
        out_specs=(hbm,) * 3,
        scratch_shapes=[pltpu.VMEM(block.shape, jnp.bfloat16), dma((4,)), dma((4,))],
        compiler_params=pltpu.CompilerParams(
            collective_id=0, has_side_effects=True, vmem_limit_bytes=32 * 1024 * 1024
        ),
        cost_estimate=pl.CostEstimate(
            flops=block.size, bytes_accessed=4 * 1024 * 1024, transcendentals=0
        ),
        name="first_halos",
    )(block)


def exchange_kernel(n_row, n_col, halos, *refs):
    block_hbm, own_grad_hbm, below_grad, beside_grad, corner_grad, sums_hbm, probe_hbm = refs[:7]
    refs = refs[7:]
    rims = ()
    new_block, out = refs[:2]
    refs = refs[2:]
    if halos:
        rims, refs = refs[:3], refs[3:]
    (
        block,
        own_grad,
        sums,
        probe,
        load,
        got_below,
        got_beside,
        got_corner,
        narrow,
        wide,
        got_col,
        own_rows,
        got_row,
        piece,
        steps,
        joined,
        got_steps,
        mixed,
        grad_send,
        grad_recv,
        halo_send,
        halo_recv,
        col_send,
        col_recv,
        row_send,
        row_recv,
        back_row_send,
        back_row_recv,
        back_col_send,
        back_col_recv,
        core_send,
        core_recv,
    ) = refs
    loads = [
        local_copy(source, target, load.at[index])
        for index, (source, target) in enumerate(
            (
                (sums_hbm, sums),
                (probe_hbm, probe),
                (block_hbm, block),
                (own_grad_hbm, own_grad),
                (below_grad.at[:, :, : mixed.shape[2]], mixed),
            )
        )
    ]
    near = Neighbours(n_row, n_col)
    row, col = near.row, near.col
    planes, size, _ = sums.shape
    chunk = size // n_col
    part = chunk // n_row
    halves = planes // 3
    comps = 2 * halves

    def along_col(step):
        return (row, lax.rem(col + step, n_col))

    def along_row(step):
        return (lax.rem(row + step, n_row), col)

    barrier = pltpu.get_barrier_semaphore()
    for step in range(1, n_col):
        greet(barrier, along_col(step))
    for step in range(1, n_row):
        greet(barrier, along_row(step))
    loads[0].wait()
    wide[...] = sums[...].astype(jnp.bfloat16)
    pl.semaphore_wait(barrier, n_col + n_row - 2)

    def started(source, target, send, recv, device):
        copy = remote(source, target, send, recv, device)
        copy.start()
        return copy

    def rows_of(index, length):
        return pl.ds(pl.multiple_of(index * length, length), length)

    first = []
    for step in range(1, n_col):
        their = lax.rem(col + step, n_col)
        first.append(
            started(
                wide.at[:, rows_of(their, chunk), :],
                got_col.at[step - 1],
                col_send.at[step - 1],
                col_recv.at[step - 1],
                along_col(step),
            )
        )
    (above, _), (left, _) = near.back()
    (under, down), (right, aside) = near.ahead()
    started_corner = jnp.logical_and(under, right)
    got_corner_here = jnp.logical_and(under, left)
    width = size
    pieces = (
        (corner_grad, got_corner, aside, started_corner, got_corner_here),
        (below_grad.at[:, :, width:], got_below.at[:, :, width:], down, under, above),
        (beside_grad, got_beside, aside, right, left),
        (mixed, got_below.at[:, :, :width], down, under, above),
    )
    grads = [
        remote(source, target, grad_send.at[index], grad_recv.at[index], device)
        for index, (source, target, device, _, _) in enumerate(pieces)
    ]
    for copy, piece_of in zip(grads[:3], pieces):
        pl.when(piece_of[3])(copy.start)
    for copy in loads[1:]:
        copy.wait()
    step_size = ALPHA / (jnp.max(probe[0] * probe[0] + probe[1] * probe[1]) + 1e-06)
    new_block[...] = block[...] - step_size * own_grad[...]

    total = sums[:, rows_of(col, chunk), :]
    for step, copy in enumerate(first):
        copy.wait_recv()
        total = total + got_col[step].astype(jnp.float32)
    for index in range(n_row):
        own_rows[index] = total[:, index * part : (index + 1) * part, :]
    second = []
    for step in range(1, n_row):
        their = lax.rem(row + step, n_row)
        second.append(
            started(
                own_rows.at[their],
                got_row.at[step - 1],
                row_send.at[step - 1],
                row_recv.at[step - 1],
                along_row(step),
            )
        )

    def mix_corner():
        grads[0].wait_recv()
        mixed[...] = (
            mixed[...].astype(jnp.float32) + got_corner[...].astype(jnp.float32)
        ).astype(jnp.bfloat16)

    pl.when(got_corner_here)(mix_corner)
    pl.when(under)(grads[3].start)
    total = own_rows[row]
    for step, copy in enumerate(second):
        copy.wait_recv()
        total = total + got_row[step]
    weight = total[2 * halves :] + 1.0
    piece[...] = jnp.concatenate(
        [total[:halves] / weight, total[halves : 2 * halves] / weight], axis=0
    )
    third = [
        started(
            piece,
            steps.at[row],
            back_row_send.at[step - 1],
            back_row_recv.at[step - 1],
            along_row(step),
        )
        for step in range(1, n_row)
    ]
    steps[row] = piece[...]
    for copy in third:
        copy.wait_recv()
    joined[...] = jnp.concatenate([steps[index] for index in range(n_row)], axis=1)
    got_steps[col] = joined[...]
    count = n_col // 2
    place, core = col // 2, lax.rem(col, 2)
    other = (row, col + 1 - 2 * core)
    across = [
        started(
            joined,
            got_steps.at[col],
            back_col_send.at[step - 1],
            back_col_recv.at[step - 1],
            (row, lax.rem(place + step, count) * 2 + core),
        )
        for step in range(1, count)
    ]
    over = [started(joined, got_steps.at[col], core_send.at[0], core_recv.at[0], other)]

    def add_below():
        grads[1].wait_recv()
        grads[3].wait_recv()
        new_block[:, :size, :] -= step_size * got_below[...].astype(jnp.float32)

    def add_beside():
        grads[2].wait_recv()
        new_block[:, :, :size] -= step_size * got_beside[...].astype(jnp.float32)

    pl.when(above)(add_below)
    pl.when(left)(add_beside)
    if halos:
        narrow[...] = new_block[...].astype(jnp.bfloat16)
        relay_halos, finish_halos = send_halos(near, narrow, rims, halo_send, halo_recv)


    for step in range(1, count):
        across[step - 1].wait_recv()
        slot = got_steps.at[lax.rem(place + count - step, count) * 2 + core]
        over.append(started(slot, slot, core_send.at[step], core_recv.at[step], other))
    if halos:
        relay_halos()
    for copy in over:
        copy.wait_recv()
    for index in range(n_col):
        rows = slice(index * chunk, (index + 1) * chunk)
        for plane in range(comps):
            comp, half = divmod(plane, halves)
            lanes = slice(half * LANES, (half + 1) * LANES)
            out[comp, rows, lanes] = probe[comp, rows, lanes] - got_steps[index, plane]
    for copy in first + second + third + across + over:
        copy.wait_send()
    for copy, piece_of in zip(grads, pieces):
        pl.when(piece_of[3])(copy.wait_send)
    if halos:
        finish_halos()


def exchange(block, own_grad, grad_rims, sums, probe_field, halos):
    n_row, n_col = lax.axis_size("row"), lax.axis_size("col")
    planes, size, _ = sums.shape
    chunk = size // n_col
    part = chunk // n_row
    comps = planes * 2 // 3
    vmem = pl.BlockSpec(memory_space=pltpu.VMEM)
    hbm = pl.BlockSpec(memory_space=pl.ANY)
    dma = pltpu.SemaphoreType.DMA
    shapes = rim_shapes(block, size)
    fresh = shapes if halos else ()
    new_block, new_probe, *rims = pl.pallas_call(
        functools.partial(exchange_kernel, n_row, n_col, halos),
        out_shape=(
            jax.ShapeDtypeStruct(block.shape, jnp.float32),
            jax.ShapeDtypeStruct(probe_field.shape, jnp.float32),
            *fresh,
        ),
        in_specs=[hbm] * 7,
        out_specs=(vmem, vmem) + (hbm,) * len(fresh),
        scratch_shapes=[
            *[pltpu.VMEM(value.shape, jnp.float32) for value in (block, own_grad, sums, probe_field)],
            dma((5,)),
            *[pltpu.VMEM(shape.shape, shape.dtype) for shape in shapes],
            pltpu.VMEM(block.shape, jnp.bfloat16),
            pltpu.VMEM(sums.shape, jnp.bfloat16),
            pltpu.VMEM((n_col - 1, planes, chunk, LANES), jnp.bfloat16),
            pltpu.VMEM((n_row, planes, part, LANES), jnp.float32),
            pltpu.VMEM((n_row - 1, planes, part, LANES), jnp.float32),
            pltpu.VMEM((comps, part, LANES), jnp.float32),
            pltpu.VMEM((n_row, comps, part, LANES), jnp.float32),
            pltpu.VMEM((comps, chunk, LANES), jnp.float32),
            pltpu.VMEM((n_col, comps, chunk, LANES), jnp.float32),
            pltpu.VMEM(shapes[2].shape, shapes[2].dtype),
            *[dma((4,))] * 4,
            dma((n_col - 1,)),
            dma((n_col - 1,)),
            dma((n_row - 1,)),
            dma((n_row - 1,)),
            dma((n_row - 1,)),
            dma((n_row - 1,)),
            dma((n_col // 2,)),
            dma((n_col // 2,)),
            dma((n_col // 2,)),
            dma((n_col // 2,)),
        ],
        compiler_params=pltpu.CompilerParams(
            collective_id=1 if halos else 2,
            has_side_effects=True,
            vmem_limit_bytes=48 * 1024 * 1024,
        ),
        cost_estimate=pl.CostEstimate(
            flops=planes * size * LANES * 4, bytes_accessed=8 * 1024 * 1024, transcendentals=0
        ),
        name="exchange",
    )(block, own_grad, *grad_rims, sums, probe_field)
    return new_block, new_probe, tuple(rims)


def local(object_field, probe_field, amplitudes, positions, live_counts):
    frame_size = probe_field.shape[-1]
    tables = chirp_blocks(frame_size)
    rims = first_halos(object_field, frame_size)
    for iteration in range(ITERS):
        planes, rows, columns = object_field.shape
        own_grad, *grad_rims, sums = frame_sums(
            object_field.reshape(planes, rows // SUBLANES, SUBLANES, columns),
            rims,
            probe_field,
            amplitudes,
            positions,
            live_counts,
            tables,
            iteration,
        )
        own_grad = own_grad.reshape(object_field.shape)
        object_field, probe_field, rims = exchange(
            object_field, own_grad, grad_rims, sums, probe_field, iteration < ITERS - 1
        )
    return (object_field, probe_field)


def solution(mesh):
    placed = (
        P(None, "row", "col"),
        P(),
        P(None, ("row", "col"), None, None),
        P(None, None, ("row", "col")),
        P(None, "col", "row"),
    )
    return jax.shard_map(
        local, mesh=mesh, in_specs=placed, out_specs=(P(None, "row", "col"), P()), check_vma=False
    )
```

```python
import functools
import math

import jax
import jax.numpy as jnp
import ml_dtypes
import numpy as np
from jax import lax
from jax.experimental import pallas as pl
from jax.experimental.pallas import tpu as pltpu
from jax.sharding import PartitionSpec as P

ITERS = 2


FLOOR = 0.3
ALPHA = 0.5
LANES = 128
SUBLANES = 8
TOGETHER = 4
STAGES = 7
MESH = pl.DeviceIdType.MESH


def chirp_blocks(frame_size):
    offset = np.arange(frame_size, dtype=np.int32)
    differ = offset[:, None] - offset[None, :]
    phase = np.pi * (differ * differ % (2 * frame_size)).astype(np.float64) / frame_size
    scale = 1.0 / math.sqrt(frame_size)
    real, imag = (np.cos(phase) * scale, np.sin(phase) * scale)
    forward = np.block([[real, -imag], [imag, real]]).astype(ml_dtypes.bfloat16)
    return jnp.asarray(forward), jnp.asarray(forward.T.copy())


def local_copy(source, target, semaphore):
    copy = pltpu.make_async_copy(source, target, semaphore)
    copy.start()
    return copy


def frames_kernel(
    iteration,
    positions,
    live,
    block,
    below,
    beside,
    corner,
    probe_hbm,
    amplitudes_hbm,
    left_hbm,
    right_hbm,
    own_grad,
    below_grad,
    beside_grad,
    corner_grad,
    sums,
    extended,
    gathered,
    below_held,
    beside_held,
    corner_held,
    probe,
    amplitudes,
    left_table,
    right_table,
    semaphores,
):
    size = probe.shape[-1]
    halves = size // LANES
    _, row_groups, _, block_columns = block.shape
    inner = (slice(None), slice(0, row_groups), slice(None), slice(0, block_columns))
    regions = (
        (below_held, below_grad, slice(row_groups, None), slice(0, block_columns)),
        (beside_held, beside_grad, slice(0, row_groups), slice(block_columns, None)),
        (corner_held, corner_grad, slice(row_groups, None), slice(block_columns, None)),
    )
    moves = (
        (below, below_held),
        (beside, beside_held),
        (corner, corner_held),
        (block, extended.at[inner]),
        (probe_hbm, probe),
        (left_hbm, left_table),
        (amplitudes_hbm.at[iteration], amplitudes),
        (right_hbm, right_table),
    )
    copies = [
        local_copy(source, target, semaphores.at[index])
        for index, (source, target) in enumerate(moves)
    ]
    gathered[...] = jnp.zeros_like(gathered)
    sums[...] = jnp.zeros_like(sums)
    for copy, (source, _, groups, lanes) in zip(copies, regions):
        copy.wait()
        planes, tall, width = source.shape
        extended[:, groups, :, lanes] = (
            source[...].astype(jnp.float32).reshape(planes, tall // SUBLANES, SUBLANES, width)
        )
    for copy in copies[len(regions) :]:
        copy.wait()
    groups = size // SUBLANES
    lane = lax.broadcasted_iota(jnp.int32, (groups + 1, SUBLANES, LANES), 2)
    sublane = lax.broadcasted_iota(jnp.int32, (groups, SUBLANES, LANES), 1)

    def dot(a, b):
        return jnp.dot(a, b, preferred_element_type=jnp.float32)

    def one_frame(slot, weight=None):
        top = positions[iteration, 0, slot]
        left = positions[iteration, 1, slot]
        column_block = left // LANES
        shift = left - column_block * LANES
        row_block = top // SUBLANES
        row_shift = top - row_block * SUBLANES
        rows = pl.ds(row_block, groups + 1)

        def columns(part):
            return pl.ds(pl.multiple_of((column_block + part) * LANES, LANES), LANES)

        patch = []
        back_shift = lax.rem(LANES - shift, LANES)
        back_row_shift = lax.rem(SUBLANES - row_shift, SUBLANES)
        keep = lane < LANES - shift
        keep_rows = sublane < SUBLANES - row_shift
        for comp in range(2):
            turned = [
                pltpu.roll(extended[comp, rows, :, columns(part)], back_shift, 2)
                for part in range(halves + 1)
            ]
            picked = []
            for part in range(halves):
                tall = pltpu.roll(
                    jnp.where(keep, turned[part], turned[part + 1]), back_row_shift, 1
                )
                picked.append(
                    jnp.where(keep_rows, tall[:groups], tall[1:]).reshape(size, LANES)
                )
            patch.append(
                jnp.concatenate(picked, axis=1).astype(jnp.bfloat16).astype(jnp.float32)
            )
        patch_real, patch_imag = patch
        probe_real, probe_imag = probe[0], probe[1]
        wave = jnp.concatenate(
            [
                probe_real * patch_real - probe_imag * patch_imag,
                probe_real * patch_imag + probe_imag * patch_real,
            ],
            axis=0,
        ).astype(jnp.bfloat16)
        yield
        near = dot(left_table[...], wave).astype(jnp.bfloat16)
        yield
        far = dot(jnp.concatenate([near[:size], near[size:]], axis=1), right_table[...])
        yield
        far_real, far_imag = far[:, :size], far[:, size:]
        power = far_real * far_real + far_imag * far_imag
        factor = 1.0 - amplitudes[slot].astype(jnp.float32) * lax.rsqrt(
            jnp.maximum(power, FLOOR * FLOOR)
        )
        misfit = jnp.concatenate([far_real * factor, far_imag * factor], axis=0).astype(
            jnp.bfloat16
        )
        yield
        back = dot(right_table[...], misfit).astype(jnp.bfloat16)
        yield
        update = dot(jnp.concatenate([back[:size], back[size:]], axis=1), left_table[...])
        yield
        update_real, update_imag = update[:, :size], update[:, size:]
        density = patch_real * patch_real + patch_imag * patch_imag
        if weight is not None:
            update_real, update_imag = update_real * weight, update_imag * weight
            density = density * weight
        terms = (
            patch_real * update_real + patch_imag * update_imag,
            patch_real * update_imag - patch_imag * update_real,
            density,
        )
        for comp, term in enumerate(terms):
            for half in range(halves):
                sums[comp * halves + half] += term[:, half * LANES : (half + 1) * LANES]
        grads = (
            probe_real * update_real + probe_imag * update_imag,
            probe_real * update_imag - probe_imag * update_real,
        )
        moved = lane >= shift
        moved_rows = sublane >= row_shift
        for comp, grad in enumerate(grads):
            grad = grad.astype(jnp.bfloat16).astype(jnp.float32)
            turned = []
            for half in range(halves):
                tall = pltpu.roll(
                    grad[:, half * LANES : (half + 1) * LANES].reshape(groups, SUBLANES, LANES),
                    row_shift,
                    1,
                )
                tall = jnp.concatenate(
                    [
                        jnp.where(moved_rows[:1], tall[:1], 0.0),
                        jnp.where(moved_rows[1:], tall[1:], tall[:-1]),
                        jnp.where(moved_rows[:1], 0.0, tall[-1:]),
                    ],
                    axis=0,
                )
                turned.append(pltpu.roll(tall, shift, 2))
            nothing = jnp.zeros_like(turned[0])
            before = [nothing] + turned
            after = turned + [nothing]
            for part in range(halves + 1):
                gathered[comp, rows, :, columns(part)] += jnp.where(
                    moved, after[part], before[part]
                )

    count = live[iteration, 0, 0]

    def together(index, carry):
        first = TOGETHER * index
        running = [one_frame(first)] + [
            one_frame(first + later, (first + later < count).astype(jnp.float32))
            for later in range(1, TOGETHER)
        ]
        for step in range(STAGES + TOGETHER - 1):
            for frame in running[: step + 1]:
                next(frame, None)
        return carry

    lax.fori_loop(0, (count + TOGETHER - 1) // TOGETHER, together, 0)
    leaving = local_copy(gathered.at[inner], own_grad, semaphores.at[0])
    for _, target, groups, lanes in regions:
        target[...] = gathered[:, groups, :, lanes].reshape(target.shape).astype(target.dtype)
    leaving.wait()


def frame_sums(block, rims, probe_field, amplitudes, positions, live, tables, iteration):
    size = probe_field.shape[-1]
    slots = amplitudes.shape[1]
    vmem = pl.BlockSpec(memory_space=pltpu.VMEM)
    smem = pl.BlockSpec(memory_space=pltpu.SMEM)
    hbm = pl.BlockSpec(memory_space=pl.ANY)
    planes, row_groups, _, columns = block.shape
    whole = (planes, row_groups + size // SUBLANES, SUBLANES, columns + size)
    held = [*rims, probe_field, amplitudes[0], *tables]
    return pl.pallas_call(
        functools.partial(frames_kernel, iteration),
        out_shape=(
            jax.ShapeDtypeStruct(block.shape, jnp.float32),
            *[jax.ShapeDtypeStruct(rim.shape, jnp.bfloat16) for rim in rims],
            jax.ShapeDtypeStruct((3 * size // LANES, size, LANES), jnp.float32),
        ),
        in_specs=[smem, smem, vmem] + [hbm] * 7,
        out_specs=(vmem,) * 5,
        scratch_shapes=[
            pltpu.VMEM(whole, jnp.float32),
            pltpu.VMEM(whole, jnp.float32),
            *[pltpu.VMEM(value.shape, value.dtype) for value in held],
            pltpu.SemaphoreType.DMA((8,)),
        ],
        compiler_params=pltpu.CompilerParams(vmem_limit_bytes=48 * 1024 * 1024),
        cost_estimate=pl.CostEstimate(
            flops=slots * 32 * size**3,
            bytes_accessed=12 * 1024 * 1024,
            transcendentals=slots * size * size,
        ),
        name="frames",
    )(positions, live, block, *rims, probe_field, amplitudes, *tables)


def remote(source, target, send, recv, device):
    return pltpu.make_async_remote_copy(
        src_ref=source,
        dst_ref=target,
        send_sem=send,
        recv_sem=recv,
        device_id=device,
        device_id_type=MESH,
    )


class Neighbours:

    def __init__(self, n_row, n_col):
        self.row, self.col = lax.axis_index("row"), lax.axis_index("col")
        self.above, self.under = self.row > 0, self.row < n_row - 1
        self.left, self.right = self.col > 0, self.col < n_col - 1

    def back(self):
        row, col = self.row, self.col
        return (
            (self.above, (row - 1, col)),
            (self.left, (row, col - 1)),
        )

    def ahead(self):
        row, col = self.row, self.col
        return (
            (self.under, (row + 1, col)),
            (self.right, (row, col + 1)),
        )


def greet(barrier, device):
    pl.semaphore_signal(barrier, inc=1, device_id=device, device_id_type=MESH)


def how_many(neighbours):
    return sum(there.astype(jnp.int32) for there, _ in neighbours)


def send_halos(near, narrow, rims, send, recv, prepare):
    below, beside, corner = rims
    _, height, size = corner.shape
    (above, up), (left, aside) = near.back()
    (under, _), (right, _) = near.ahead()
    first, rest = slice(0, size), slice(size, None)
    pieces = (
        (narrow.at[:, :height, first], below.at[:, :, first], up),
        (narrow.at[:, :height, rest], below.at[:, :, rest], up),
        (narrow.at[:, :, first], beside, aside),
        (below.at[:, :, first], corner, aside),
    )
    sent = [
        remote(source, target, send.at[index], recv.at[index], device)
        for index, (source, target, device) in enumerate(pieces)
    ]
    relays = jnp.logical_and(under, left)
    relayed = jnp.logical_and(under, right)
    for copy in sent[:2]:
        pl.when(above)(copy.start)
    prepare()
    pl.when(left)(sent[2].start)

    def relay():
        pl.when(under)(sent[0].wait_recv)
        pl.when(relays)(sent[3].start)

    def finish():
        for copy, there in zip(sent[1:], (under, right, relayed)):
            pl.when(there)(copy.wait_recv)
        for copy, there in zip(sent, (above, above, left, relays)):
            pl.when(there)(copy.wait_send)

    return relay, finish


def halo_kernel(
    n_row, n_col, block_hbm, below, beside, corner, block, narrow, load, send, recv
):
    _, height, size = corner.shape
    parts = (slice(0, height), slice(height, None))
    loads = [
        local_copy(block_hbm.at[:, rows], block.at[:, rows], load.at[index])
        for index, rows in enumerate(parts)
    ]
    near = Neighbours(n_row, n_col)
    barrier = pltpu.get_barrier_semaphore()
    for there, device in near.back() + near.ahead():
        pl.when(there)(functools.partial(greet, barrier, device))
    loads[0].wait()
    narrow[:, parts[0]] = block[:, parts[0]].astype(jnp.bfloat16)
    pl.semaphore_wait(barrier, how_many(near.back() + near.ahead()))

    def rest():
        loads[1].wait()
        narrow[:, parts[1]] = block[:, parts[1]].astype(jnp.bfloat16)

    relay, finish = send_halos(near, narrow, (below, beside, corner), send, recv, rest)
    relay()
    finish()


def rim_shapes(block, size):
    planes, rows, columns = block.shape
    return tuple(
        jax.ShapeDtypeStruct(shape, jnp.bfloat16)
        for shape in ((planes, size, columns), (planes, rows, size), (planes, size, size))
    )


def first_halos(block, size):
    n_row, n_col = lax.axis_size("row"), lax.axis_size("col")
    hbm = pl.BlockSpec(memory_space=pl.ANY)
    dma = pltpu.SemaphoreType.DMA
    return pl.pallas_call(
        functools.partial(halo_kernel, n_row, n_col),
        out_shape=rim_shapes(block, size),
        in_specs=[hbm],
        out_specs=(hbm,) * 3,
        scratch_shapes=[
            pltpu.VMEM(block.shape, jnp.float32),
            pltpu.VMEM(block.shape, jnp.bfloat16),
            dma((2,)),
            dma((4,)),
            dma((4,)),
        ],
        compiler_params=pltpu.CompilerParams(
            collective_id=0, has_side_effects=True, vmem_limit_bytes=32 * 1024 * 1024
        ),
        cost_estimate=pl.CostEstimate(
            flops=block.size, bytes_accessed=4 * 1024 * 1024, transcendentals=0
        ),
        name="first_halos",
    )(block)


def exchange_kernel(n_row, n_col, halos, *refs):
    block_hbm, own_grad_hbm, below_grad, beside_grad, corner_grad, sums_hbm, probe_hbm = refs[:7]
    refs = refs[7:]
    rims = ()
    new_block, out = refs[:2]
    refs = refs[2:]
    if halos:
        rims, refs = refs[:3], refs[3:]
    (
        block,
        own_grad,
        sums,
        probe,
        load,
        got_below,
        got_beside,
        got_corner,
        narrow,
        wide,
        got_col,
        own_rows,
        got_row,
        piece,
        steps,
        joined,
        got_steps,
        mixed,
        grad_send,
        grad_recv,
        halo_send,
        halo_recv,
        col_send,
        col_recv,
        row_send,
        row_recv,
        back_row_send,
        back_row_recv,
        back_col_send,
        back_col_recv,
        core_send,
        core_recv,
    ) = refs
    loads = [
        local_copy(source, target, load.at[index])
        for index, (source, target) in enumerate(
            (
                (sums_hbm, sums),
                (probe_hbm, probe),
                (block_hbm, block),
                (own_grad_hbm, own_grad),
                (below_grad.at[:, :, : mixed.shape[2]], mixed),
            )
        )
    ]
    near = Neighbours(n_row, n_col)
    row, col = near.row, near.col
    planes, size, _ = sums.shape
    chunk = size // n_col
    part = chunk // n_row
    halves = planes // 3
    comps = 2 * halves

    def along_col(step):
        return (row, lax.rem(col + step, n_col))

    def along_row(step):
        return (lax.rem(row + step, n_row), col)

    barrier = pltpu.get_barrier_semaphore()
    for step in range(1, n_col):
        greet(barrier, along_col(step))
    for step in range(1, n_row):
        greet(barrier, along_row(step))
    loads[0].wait()
    wide[...] = sums[...].astype(jnp.bfloat16)
    pl.semaphore_wait(barrier, n_col + n_row - 2)

    def started(source, target, send, recv, device):
        copy = remote(source, target, send, recv, device)
        copy.start()
        return copy

    def rows_of(index, length):
        return pl.ds(pl.multiple_of(index * length, length), length)

    first = []
    for step in range(1, n_col):
        their = lax.rem(col + step, n_col)
        first.append(
            started(
                wide.at[:, rows_of(their, chunk), :],
                got_col.at[step - 1],
                col_send.at[step - 1],
                col_recv.at[step - 1],
                along_col(step),
            )
        )
    (above, _), (left, _) = near.back()
    (under, down), (right, aside) = near.ahead()
    started_corner = jnp.logical_and(under, right)
    got_corner_here = jnp.logical_and(under, left)
    width = size
    pieces = (
        (corner_grad, got_corner, aside, started_corner, got_corner_here),
        (below_grad.at[:, :, width:], got_below.at[:, :, width:], down, under, above),
        (beside_grad, got_beside, aside, right, left),
        (mixed, got_below.at[:, :, :width], down, under, above),
    )
    grads = [
        remote(source, target, grad_send.at[index], grad_recv.at[index], device)
        for index, (source, target, device, _, _) in enumerate(pieces)
    ]
    for copy, piece_of in zip(grads[:2], pieces):
        pl.when(piece_of[3])(copy.start)
    for copy in loads[1:]:
        copy.wait()
    step_size = ALPHA / (jnp.max(probe[0] * probe[0] + probe[1] * probe[1]) + 1e-06)
    new_block[...] = block[...] - step_size * own_grad[...]

    total = sums[:, rows_of(col, chunk), :]
    for step, copy in enumerate(first):
        copy.wait_recv()
        total = total + got_col[step].astype(jnp.float32)
    for index in range(n_row):
        own_rows[index] = total[:, index * part : (index + 1) * part, :]
    second = []
    for step in range(1, n_row):
        their = lax.rem(row + step, n_row)
        second.append(
            started(
                own_rows.at[their],
                got_row.at[step - 1],
                row_send.at[step - 1],
                row_recv.at[step - 1],
                along_row(step),
            )
        )

    pl.when(right)(grads[2].start)

    def mix_corner():
        grads[0].wait_recv()
        mixed[...] = (
            mixed[...].astype(jnp.float32) + got_corner[...].astype(jnp.float32)
        ).astype(jnp.bfloat16)

    pl.when(got_corner_here)(mix_corner)
    pl.when(under)(grads[3].start)
    total = own_rows[row]
    for step, copy in enumerate(second):
        copy.wait_recv()
        total = total + got_row[step]
    weight = total[2 * halves :] + 1.0
    piece[...] = jnp.concatenate(
        [total[:halves] / weight, total[halves : 2 * halves] / weight], axis=0
    )
    third = [
        started(
            piece,
            steps.at[row],
            back_row_send.at[step - 1],
            back_row_recv.at[step - 1],
            along_row(step),
        )
        for step in range(1, n_row)
    ]
    steps[row] = piece[...]
    for copy in third:
        copy.wait_recv()
    joined[...] = jnp.concatenate([steps[index] for index in range(n_row)], axis=1)
    got_steps[col] = joined[...]
    count = n_col // 2
    place, core = col // 2, lax.rem(col, 2)
    other = (row, col + 1 - 2 * core)
    across = [
        started(
            joined,
            got_steps.at[col],
            back_col_send.at[step - 1],
            back_col_recv.at[step - 1],
            (row, lax.rem(place + step, count) * 2 + core),
        )
        for step in range(1, count)
    ]
    over = [started(joined, got_steps.at[col], core_send.at[0], core_recv.at[0], other)]

    def add_below():
        grads[1].wait_recv()
        grads[3].wait_recv()
        new_block[:, :size, :] -= step_size * got_below[...].astype(jnp.float32)

    def add_beside():
        grads[2].wait_recv()
        new_block[:, :, :size] -= step_size * got_beside[...].astype(jnp.float32)

    pl.when(left)(add_beside)
    if halos:
        narrow[:, size:] = new_block[:, size:].astype(jnp.bfloat16)
    pl.when(above)(add_below)
    if halos:
        narrow[:, :size] = new_block[:, :size].astype(jnp.bfloat16)
        relay_halos, finish_halos = send_halos(
            near, narrow, rims, halo_send, halo_recv, lambda: None
        )

    for step in range(1, count):
        across[step - 1].wait_recv()
        slot = got_steps.at[lax.rem(place + count - step, count) * 2 + core]
        over.append(started(slot, slot, core_send.at[step], core_recv.at[step], other))
    if halos:
        relay_halos()
    for copy in over:
        copy.wait_recv()
    for index in range(n_col):
        rows = slice(index * chunk, (index + 1) * chunk)
        for plane in range(comps):
            comp, half = divmod(plane, halves)
            lanes = slice(half * LANES, (half + 1) * LANES)
            out[comp, rows, lanes] = probe[comp, rows, lanes] - got_steps[index, plane]
    for copy in first + second + third + across + over:
        copy.wait_send()
    for copy, piece_of in zip(grads, pieces):
        pl.when(piece_of[3])(copy.wait_send)
    if halos:
        finish_halos()


def exchange(block, own_grad, grad_rims, sums, probe_field, halos):
    n_row, n_col = lax.axis_size("row"), lax.axis_size("col")
    planes, size, _ = sums.shape
    chunk = size // n_col
    part = chunk // n_row
    comps = planes * 2 // 3
    vmem = pl.BlockSpec(memory_space=pltpu.VMEM)
    hbm = pl.BlockSpec(memory_space=pl.ANY)
    dma = pltpu.SemaphoreType.DMA
    shapes = rim_shapes(block, size)
    fresh = shapes if halos else ()
    new_block, new_probe, *rims = pl.pallas_call(
        functools.partial(exchange_kernel, n_row, n_col, halos),
        out_shape=(
            jax.ShapeDtypeStruct(block.shape, jnp.float32),
            jax.ShapeDtypeStruct(probe_field.shape, jnp.float32),
            *fresh,
        ),
        in_specs=[hbm] * 7,
        out_specs=(vmem, vmem) + (hbm,) * len(fresh),
        scratch_shapes=[
            *[pltpu.VMEM(value.shape, jnp.float32) for value in (block, own_grad, sums, probe_field)],
            dma((5,)),
            *[pltpu.VMEM(shape.shape, shape.dtype) for shape in shapes],
            pltpu.VMEM(block.shape, jnp.bfloat16),
            pltpu.VMEM(sums.shape, jnp.bfloat16),
            pltpu.VMEM((n_col - 1, planes, chunk, LANES), jnp.bfloat16),
            pltpu.VMEM((n_row, planes, part, LANES), jnp.float32),
            pltpu.VMEM((n_row - 1, planes, part, LANES), jnp.float32),
            pltpu.VMEM((comps, part, LANES), jnp.float32),
            pltpu.VMEM((n_row, comps, part, LANES), jnp.float32),
            pltpu.VMEM((comps, chunk, LANES), jnp.float32),
            pltpu.VMEM((n_col, comps, chunk, LANES), jnp.float32),
            pltpu.VMEM(shapes[2].shape, shapes[2].dtype),
            *[dma((4,))] * 4,
            dma((n_col - 1,)),
            dma((n_col - 1,)),
            dma((n_row - 1,)),
            dma((n_row - 1,)),
            dma((n_row - 1,)),
            dma((n_row - 1,)),
            dma((n_col // 2,)),
            dma((n_col // 2,)),
            dma((n_col // 2,)),
            dma((n_col // 2,)),
        ],
        compiler_params=pltpu.CompilerParams(
            collective_id=1 if halos else 2,
            has_side_effects=True,
            vmem_limit_bytes=48 * 1024 * 1024,
        ),
        cost_estimate=pl.CostEstimate(
            flops=planes * size * LANES * 4, bytes_accessed=8 * 1024 * 1024, transcendentals=0
        ),
        name="exchange",
    )(block, own_grad, *grad_rims, sums, probe_field)
    return new_block, new_probe, tuple(rims)


def local(object_field, probe_field, amplitudes, positions, live_counts):
    frame_size = probe_field.shape[-1]
    tables = chirp_blocks(frame_size)
    rims = first_halos(object_field, frame_size)
    for iteration in range(ITERS):
        planes, rows, columns = object_field.shape
        own_grad, *grad_rims, sums = frame_sums(
            object_field.reshape(planes, rows // SUBLANES, SUBLANES, columns),
            rims,
            probe_field,
            amplitudes,
            positions,
            live_counts,
            tables,
            iteration,
        )
        own_grad = own_grad.reshape(object_field.shape)
        object_field, probe_field, rims = exchange(
            object_field, own_grad, grad_rims, sums, probe_field, iteration < ITERS - 1
        )
    return (object_field, probe_field)


def solution(mesh):
    placed = (
        P(None, "row", "col"),
        P(),
        P(None, ("row", "col"), None, None),
        P(None, None, ("row", "col")),
        P(None, "col", "row"),
    )
    return jax.shard_map(
        local, mesh=mesh, in_specs=placed, out_specs=(P(None, "row", "col"), P()), check_vma=False
    )
```

```python
import functools
import math

import jax
import jax.numpy as jnp
import ml_dtypes
import numpy as np
from jax import lax
from jax.experimental import pallas as pl
from jax.experimental.pallas import tpu as pltpu
from jax.sharding import PartitionSpec as P

ITERS = 2


FLOOR = 0.3
ALPHA = 0.5
LANES = 128
SUBLANES = 8
TOGETHER = 4
STAGES = 7
MESH = pl.DeviceIdType.MESH


def chirp_blocks(frame_size):
    offset = np.arange(frame_size, dtype=np.int32)
    differ = offset[:, None] - offset[None, :]
    phase = np.pi * (differ * differ % (2 * frame_size)).astype(np.float64) / frame_size
    scale = 1.0 / math.sqrt(frame_size)
    real, imag = (np.cos(phase) * scale, np.sin(phase) * scale)
    forward = np.block([[real, -imag], [imag, real]]).astype(ml_dtypes.bfloat16)
    return jnp.asarray(forward), jnp.asarray(forward.T.copy())


def local_copy(source, target, semaphore):
    copy = pltpu.make_async_copy(source, target, semaphore)
    copy.start()
    return copy


def frames_kernel(
    iteration,
    positions,
    live,
    block,
    below,
    beside,
    corner,
    probe_hbm,
    amplitudes_hbm,
    left_hbm,
    right_hbm,
    own_grad,
    below_grad,
    beside_grad,
    corner_grad,
    sums,
    extended,
    gathered,
    below_held,
    beside_held,
    corner_held,
    probe,
    amplitudes,
    left_table,
    right_table,
    semaphores,
):
    size = probe.shape[-1]
    halves = size // LANES
    _, row_groups, _, block_columns = block.shape
    inner = (slice(None), slice(0, row_groups), slice(None), slice(0, block_columns))
    regions = (
        (below_held, below_grad, slice(row_groups, None), slice(0, block_columns)),
        (beside_held, beside_grad, slice(0, row_groups), slice(block_columns, None)),
        (corner_held, corner_grad, slice(row_groups, None), slice(block_columns, None)),
    )
    moves = (
        (below, below_held),
        (beside, beside_held),
        (corner, corner_held),
        (block, extended.at[inner]),
        (probe_hbm, probe),
        (left_hbm, left_table),
        (amplitudes_hbm.at[iteration], amplitudes),
        (right_hbm, right_table),
    )
    copies = [
        local_copy(source, target, semaphores.at[index])
        for index, (source, target) in enumerate(moves)
    ]
    gathered[...] = jnp.zeros_like(gathered)
    sums[...] = jnp.zeros_like(sums)
    for copy, (source, _, groups, lanes) in zip(copies, regions):
        copy.wait()
        planes, tall, width = source.shape
        extended[:, groups, :, lanes] = (
            source[...].astype(jnp.float32).reshape(planes, tall // SUBLANES, SUBLANES, width)
        )
    for copy in copies[len(regions) :]:
        copy.wait()
    groups = size // SUBLANES
    lane = lax.broadcasted_iota(jnp.int32, (groups + 1, SUBLANES, LANES), 2)
    sublane = lax.broadcasted_iota(jnp.int32, (groups, SUBLANES, LANES), 1)

    def dot(a, b):
        return jnp.dot(a, b, preferred_element_type=jnp.float32)

    def one_frame(slot, weight=None):
        top = positions[iteration, 0, slot]
        left = positions[iteration, 1, slot]
        column_block = left // LANES
        shift = left - column_block * LANES
        row_block = top // SUBLANES
        row_shift = top - row_block * SUBLANES
        rows = pl.ds(row_block, groups + 1)

        def columns(part):
            return pl.ds(pl.multiple_of((column_block + part) * LANES, LANES), LANES)

        patch = []
        back_shift = lax.rem(LANES - shift, LANES)
        back_row_shift = lax.rem(SUBLANES - row_shift, SUBLANES)
        keep = lane < LANES - shift
        keep_rows = sublane < SUBLANES - row_shift
        for comp in range(2):
            turned = [
                pltpu.roll(extended[comp, rows, :, columns(part)], back_shift, 2)
                for part in range(halves + 1)
            ]
            picked = []
            for part in range(halves):
                tall = pltpu.roll(
                    jnp.where(keep, turned[part], turned[part + 1]), back_row_shift, 1
                )
                picked.append(
                    jnp.where(keep_rows, tall[:groups], tall[1:]).reshape(size, LANES)
                )
            patch.append(
                jnp.concatenate(picked, axis=1).astype(jnp.bfloat16).astype(jnp.float32)
            )
        patch_real, patch_imag = patch
        probe_real, probe_imag = probe[0], probe[1]
        wave = jnp.concatenate(
            [
                probe_real * patch_real - probe_imag * patch_imag,
                probe_real * patch_imag + probe_imag * patch_real,
            ],
            axis=0,
        ).astype(jnp.bfloat16)
        yield
        near = dot(left_table[...], wave).astype(jnp.bfloat16)
        yield
        far = dot(jnp.concatenate([near[:size], near[size:]], axis=1), right_table[...])
        yield
        far_real, far_imag = far[:, :size], far[:, size:]
        power = far_real * far_real + far_imag * far_imag
        factor = 1.0 - amplitudes[slot].astype(jnp.float32) * lax.rsqrt(
            jnp.maximum(power, FLOOR * FLOOR)
        )
        misfit = jnp.concatenate([far_real * factor, far_imag * factor], axis=0).astype(
            jnp.bfloat16
        )
        yield
        back = dot(right_table[...], misfit).astype(jnp.bfloat16)
        yield
        update = dot(jnp.concatenate([back[:size], back[size:]], axis=1), left_table[...])
        yield
        update_real, update_imag = update[:, :size], update[:, size:]
        density = patch_real * patch_real + patch_imag * patch_imag
        if weight is not None:
            update_real, update_imag = update_real * weight, update_imag * weight
            density = density * weight
        terms = (
            patch_real * update_real + patch_imag * update_imag,
            patch_real * update_imag - patch_imag * update_real,
            density,
        )
        for comp, term in enumerate(terms):
            for half in range(halves):
                sums[comp * halves + half] += term[:, half * LANES : (half + 1) * LANES]
        grads = (
            probe_real * update_real + probe_imag * update_imag,
            probe_real * update_imag - probe_imag * update_real,
        )
        moved = lane >= shift
        moved_rows = sublane >= row_shift
        for comp, grad in enumerate(grads):
            grad = grad.astype(jnp.bfloat16).astype(jnp.float32)
            turned = []
            for half in range(halves):
                tall = pltpu.roll(
                    grad[:, half * LANES : (half + 1) * LANES].reshape(groups, SUBLANES, LANES),
                    row_shift,
                    1,
                )
                tall = jnp.concatenate(
                    [
                        jnp.where(moved_rows[:1], tall[:1], 0.0),
                        jnp.where(moved_rows[1:], tall[1:], tall[:-1]),
                        jnp.where(moved_rows[:1], 0.0, tall[-1:]),
                    ],
                    axis=0,
                )
                turned.append(pltpu.roll(tall, shift, 2))
            nothing = jnp.zeros_like(turned[0])
            before = [nothing] + turned
            after = turned + [nothing]
            for part in range(halves + 1):
                gathered[comp, rows, :, columns(part)] += jnp.where(
                    moved, after[part], before[part]
                )

    count = live[iteration, 0, 0]

    def together(index, carry):
        first = TOGETHER * index
        running = [one_frame(first)] + [
            one_frame(first + later, (first + later < count).astype(jnp.float32))
            for later in range(1, TOGETHER)
        ]
        for step in range(STAGES + TOGETHER - 1):
            for frame in running[: step + 1]:
                next(frame, None)
        return carry

    lax.fori_loop(0, (count + TOGETHER - 1) // TOGETHER, together, 0)
    leaving = local_copy(gathered.at[inner], own_grad, semaphores.at[0])
    for _, target, groups, lanes in regions:
        target[...] = gathered[:, groups, :, lanes].reshape(target.shape).astype(target.dtype)
    leaving.wait()


def frame_sums(block, rims, probe_field, amplitudes, positions, live, tables, iteration):
    size = probe_field.shape[-1]
    slots = amplitudes.shape[1]
    vmem = pl.BlockSpec(memory_space=pltpu.VMEM)
    smem = pl.BlockSpec(memory_space=pltpu.SMEM)
    hbm = pl.BlockSpec(memory_space=pl.ANY)
    planes, row_groups, _, columns = block.shape
    whole = (planes, row_groups + size // SUBLANES, SUBLANES, columns + size)
    held = [*rims, probe_field, amplitudes[0], *tables]
    return pl.pallas_call(
        functools.partial(frames_kernel, iteration),
        out_shape=(
            jax.ShapeDtypeStruct(block.shape, jnp.float32),
            *[jax.ShapeDtypeStruct(rim.shape, jnp.bfloat16) for rim in rims],
            jax.ShapeDtypeStruct((3 * size // LANES, size, LANES), jnp.float32),
        ),
        in_specs=[smem, smem] + [hbm] * 8,
        out_specs=(vmem,) * 5,
        scratch_shapes=[
            pltpu.VMEM(whole, jnp.float32),
            pltpu.VMEM(whole, jnp.float32),
            *[pltpu.VMEM(value.shape, value.dtype) for value in held],
            pltpu.SemaphoreType.DMA((8,)),
        ],
        compiler_params=pltpu.CompilerParams(vmem_limit_bytes=48 * 1024 * 1024),
        cost_estimate=pl.CostEstimate(
            flops=slots * 32 * size**3,
            bytes_accessed=12 * 1024 * 1024,
            transcendentals=slots * size * size,
        ),
        name="frames",
    )(positions, live, block, *rims, probe_field, amplitudes, *tables)


def remote(source, target, send, recv, device):
    return pltpu.make_async_remote_copy(
        src_ref=source,
        dst_ref=target,
        send_sem=send,
        recv_sem=recv,
        device_id=device,
        device_id_type=MESH,
    )


class Neighbours:

    def __init__(self, n_row, n_col):
        self.row, self.col = lax.axis_index("row"), lax.axis_index("col")
        self.above, self.under = self.row > 0, self.row < n_row - 1
        self.left, self.right = self.col > 0, self.col < n_col - 1

    def back(self):
        row, col = self.row, self.col
        return (
            (self.above, (row - 1, col)),
            (self.left, (row, col - 1)),
        )

    def ahead(self):
        row, col = self.row, self.col
        return (
            (self.under, (row + 1, col)),
            (self.right, (row, col + 1)),
        )


def greet(barrier, device):
    pl.semaphore_signal(barrier, inc=1, device_id=device, device_id_type=MESH)


def how_many(neighbours):
    return sum(there.astype(jnp.int32) for there, _ in neighbours)


def send_halos(near, narrow, rims, send, recv, prepare):
    below, beside, corner = rims
    _, height, size = corner.shape
    (above, up), (left, aside) = near.back()
    (under, _), (right, _) = near.ahead()
    first, rest = slice(0, size), slice(size, None)
    pieces = (
        (narrow.at[:, :height, first], below.at[:, :, first], up),
        (narrow.at[:, :height, rest], below.at[:, :, rest], up),
        (narrow.at[:, :, first], beside, aside),
        (below.at[:, :, first], corner, aside),
    )
    sent = [
        remote(source, target, send.at[index], recv.at[index], device)
        for index, (source, target, device) in enumerate(pieces)
    ]
    relays = jnp.logical_and(under, left)
    relayed = jnp.logical_and(under, right)
    for copy in sent[:2]:
        pl.when(above)(copy.start)
    prepare()
    pl.when(left)(sent[2].start)

    def relay():
        pl.when(under)(sent[0].wait_recv)
        pl.when(relays)(sent[3].start)

    def finish():
        for copy, there in zip(sent[1:], (under, right, relayed)):
            pl.when(there)(copy.wait_recv)
        for copy, there in zip(sent, (above, above, left, relays)):
            pl.when(there)(copy.wait_send)

    return relay, finish


def halo_kernel(
    n_row, n_col, block_hbm, below, beside, corner, block, narrow, load, send, recv
):
    _, height, size = corner.shape
    parts = (slice(0, height), slice(height, None))
    loads = [
        local_copy(block_hbm.at[:, rows], block.at[:, rows], load.at[index])
        for index, rows in enumerate(parts)
    ]
    near = Neighbours(n_row, n_col)
    barrier = pltpu.get_barrier_semaphore()
    for there, device in near.back() + near.ahead():
        pl.when(there)(functools.partial(greet, barrier, device))
    loads[0].wait()
    narrow[:, parts[0]] = block[:, parts[0]].astype(jnp.bfloat16)
    pl.semaphore_wait(barrier, how_many(near.back() + near.ahead()))

    def rest():
        loads[1].wait()
        narrow[:, parts[1]] = block[:, parts[1]].astype(jnp.bfloat16)

    relay, finish = send_halos(near, narrow, (below, beside, corner), send, recv, rest)
    relay()
    finish()


def rim_shapes(block, size):
    planes, rows, columns = block.shape
    return tuple(
        jax.ShapeDtypeStruct(shape, jnp.bfloat16)
        for shape in ((planes, size, columns), (planes, rows, size), (planes, size, size))
    )


def first_halos(block, size):
    n_row, n_col = lax.axis_size("row"), lax.axis_size("col")
    hbm = pl.BlockSpec(memory_space=pl.ANY)
    dma = pltpu.SemaphoreType.DMA
    return pl.pallas_call(
        functools.partial(halo_kernel, n_row, n_col),
        out_shape=rim_shapes(block, size),
        in_specs=[pl.BlockSpec(memory_space=pltpu.HBM)],
        out_specs=(hbm,) * 3,
        scratch_shapes=[
            pltpu.VMEM(block.shape, jnp.float32),
            pltpu.VMEM(block.shape, jnp.bfloat16),
            dma((2,)),
            dma((4,)),
            dma((4,)),
        ],
        compiler_params=pltpu.CompilerParams(
            collective_id=0, has_side_effects=True, vmem_limit_bytes=32 * 1024 * 1024
        ),
        cost_estimate=pl.CostEstimate(
            flops=block.size, bytes_accessed=4 * 1024 * 1024, transcendentals=0
        ),
        name="first_halos",
    )(block)


def exchange_kernel(n_row, n_col, halos, *refs):
    block_hbm, own_grad, below_grad, beside_grad, corner_grad, sums, probe = refs[:7]
    refs = refs[7:]
    rims = ()
    block_out, out = refs[:2]
    refs = refs[2:]
    if halos:
        rims, refs = refs[:3], refs[3:]
    new_block = block_out
    if halos:
        new_block, refs = refs[0], refs[1:]
    (
        block,
        load,
        got_below,
        got_beside,
        got_corner,
        narrow,
        wide,
        got_col,
        kept,
        own_rows,
        got_row,
        piece,
        steps,
        joined,
        got_steps,
        mixed,
        grad_send,
        grad_recv,
        halo_send,
        halo_recv,
        col_send,
        col_recv,
        row_send,
        row_recv,
        back_row_send,
        back_row_recv,
        back_col_send,
        back_col_recv,
        core_send,
        core_recv,
    ) = refs
    loads = [
        local_copy(source, target, load.at[index])
        for index, (source, target) in enumerate(
            ((block_hbm, block), (below_grad.at[:, :, : mixed.shape[2]], mixed))
        )
    ]
    near = Neighbours(n_row, n_col)
    row, col = near.row, near.col
    planes, size, _ = sums.shape
    chunk = size // n_col
    part = chunk // n_row
    halves = planes // 3
    comps = 2 * halves

    def along_col(step):
        return (row, lax.rem(col + step, n_col))

    def along_row(step):
        return (lax.rem(row + step, n_row), col)

    barrier = pltpu.get_barrier_semaphore()
    for step in range(1, n_col):
        greet(barrier, along_col(step))
    for step in range(1, n_row):
        greet(barrier, along_row(step))
    wide[...] = sums[...].astype(jnp.bfloat16)
    pl.semaphore_wait(barrier, n_col + n_row - 2)

    def started(source, target, send, recv, device):
        copy = remote(source, target, send, recv, device)
        copy.start()
        return copy

    def rows_of(index, length):
        return pl.ds(pl.multiple_of(index * length, length), length)

    first = []
    for step in range(1, n_col):
        their = lax.rem(col + step, n_col)
        first.append(
            started(
                wide.at[:, rows_of(their, chunk), :],
                got_col.at[step - 1],
                col_send.at[step - 1],
                col_recv.at[step - 1],
                along_col(step),
            )
        )
    (above, _), (left, _) = near.back()
    (under, down), (right, aside) = near.ahead()
    started_corner = jnp.logical_and(under, right)
    got_corner_here = jnp.logical_and(under, left)
    width = size
    pieces = (
        (corner_grad, got_corner, aside, started_corner, got_corner_here),
        (below_grad.at[:, :, width:], got_below.at[:, :, width:], down, under, above),
        (beside_grad, got_beside, aside, right, left),
        (mixed, got_below.at[:, :, :width], down, under, above),
    )
    grads = [
        remote(source, target, grad_send.at[index], grad_recv.at[index], device)
        for index, (source, target, device, _, _) in enumerate(pieces)
    ]
    for copy, piece_of in zip(grads[:2], pieces):
        pl.when(piece_of[3])(copy.start)
    for copy in loads:
        copy.wait()
    step_size = ALPHA / (jnp.max(probe[0] * probe[0] + probe[1] * probe[1]) + 1e-06)
    new_block[...] = block[...] - step_size * own_grad[...]

    total = sums[:, rows_of(col, chunk), :]
    for step, copy in enumerate(first):
        copy.wait_recv()
        total = total + got_col[step].astype(jnp.float32)
    spare = own_rows.shape[1] - planes * part
    for index in range(n_row):
        rows = slice(index * part, (index + 1) * part)
        flat = jnp.concatenate([total[plane, rows] for plane in range(planes)], axis=0)
        kept[index] = flat
        if spare:
            flat = jnp.concatenate([flat, jnp.zeros((spare, LANES), jnp.float32)], axis=0)
        own_rows[index] = flat.astype(jnp.bfloat16)
    second = []
    for step in range(1, n_row):
        their = lax.rem(row + step, n_row)
        second.append(
            started(
                own_rows.at[their],
                got_row.at[step - 1],
                row_send.at[step - 1],
                row_recv.at[step - 1],
                along_row(step),
            )
        )

    pl.when(right)(grads[2].start)

    def mix_corner():
        grads[0].wait_recv()
        mixed[...] = (
            mixed[...].astype(jnp.float32) + got_corner[...].astype(jnp.float32)
        ).astype(jnp.bfloat16)

    pl.when(got_corner_here)(mix_corner)
    pl.when(under)(grads[3].start)
    total = kept[row]
    for step, copy in enumerate(second):
        copy.wait_recv()
        total = total + got_row[step].astype(jnp.float32)[: planes * part]
    third_part = halves * part
    weight = total[2 * third_part :] + 1.0
    piece[...] = jnp.concatenate(
        [total[:third_part] / weight, total[third_part : 2 * third_part] / weight], axis=0
    )
    third = [
        started(
            piece,
            steps.at[row],
            back_row_send.at[step - 1],
            back_row_recv.at[step - 1],
            along_row(step),
        )
        for step in range(1, n_row)
    ]
    steps[row] = piece[...]
    for copy in third:
        copy.wait_recv()
    for plane in range(comps):
        rows = slice(plane * part, (plane + 1) * part)
        joined[plane] = jnp.concatenate([steps[index, rows] for index in range(n_row)], axis=0)
    got_steps[col] = joined[...]
    count = n_col // 2
    place, core = col // 2, lax.rem(col, 2)
    other = (row, col + 1 - 2 * core)
    across = [
        started(
            joined,
            got_steps.at[col],
            back_col_send.at[step - 1],
            back_col_recv.at[step - 1],
            (row, lax.rem(place + step, count) * 2 + core),
        )
        for step in range(1, count)
    ]
    over = [started(joined, got_steps.at[col], core_send.at[0], core_recv.at[0], other)]

    def add_below():
        grads[1].wait_recv()
        grads[3].wait_recv()
        new_block[:, :size, :] -= step_size * got_below[...].astype(jnp.float32)

    def add_beside():
        grads[2].wait_recv()
        new_block[:, :, :size] -= step_size * got_beside[...].astype(jnp.float32)

    pl.when(left)(add_beside)
    if halos:
        narrow[:, size:] = new_block[:, size:].astype(jnp.bfloat16)
    pl.when(above)(add_below)
    if halos:
        narrow[:, :size] = new_block[:, :size].astype(jnp.bfloat16)
        relay_halos, finish_halos = send_halos(
            near, narrow, rims, halo_send, halo_recv, lambda: None
        )
        leaving = local_copy(new_block, block_out, load.at[2])

    for step in range(1, count):
        across[step - 1].wait_recv()
        slot = got_steps.at[lax.rem(place + count - step, count) * 2 + core]
        over.append(started(slot, slot, core_send.at[step], core_recv.at[step], other))
    if halos:
        relay_halos()
    for copy in over:
        copy.wait_recv()
    for index in range(n_col):
        rows = slice(index * chunk, (index + 1) * chunk)
        for plane in range(comps):
            comp, half = divmod(plane, halves)
            lanes = slice(half * LANES, (half + 1) * LANES)
            out[comp, rows, lanes] = probe[comp, rows, lanes] - got_steps[index, plane]
    for copy in first + second + third + across + over:
        copy.wait_send()
    for copy, piece_of in zip(grads, pieces):
        pl.when(piece_of[3])(copy.wait_send)
    if halos:
        finish_halos()
        leaving.wait()


def exchange(block, own_grad, grad_rims, sums, probe_field, halos):
    n_row, n_col = lax.axis_size("row"), lax.axis_size("col")
    planes, size, _ = sums.shape
    chunk = size // n_col
    part = chunk // n_row
    comps = planes * 2 // 3
    padded = -(-planes * part // 16) * 16
    vmem = pl.BlockSpec(memory_space=pltpu.VMEM)
    hbm = pl.BlockSpec(memory_space=pl.ANY)
    dma = pltpu.SemaphoreType.DMA
    shapes = rim_shapes(block, size)
    fresh = shapes if halos else ()
    new_block, new_probe, *rims = pl.pallas_call(
        functools.partial(exchange_kernel, n_row, n_col, halos),
        out_shape=(
            jax.ShapeDtypeStruct(block.shape, jnp.float32),
            jax.ShapeDtypeStruct(probe_field.shape, jnp.float32),
            *fresh,
        ),
        in_specs=[hbm, vmem, hbm, hbm, hbm, vmem, vmem],
        out_specs=(pl.BlockSpec(memory_space=pltpu.HBM) if halos else vmem, vmem)
        + (hbm,) * len(fresh),
        scratch_shapes=[
            *[pltpu.VMEM(block.shape, jnp.float32)] * (2 if halos else 1),
            dma((3,)),
            *[pltpu.VMEM(shape.shape, shape.dtype) for shape in shapes],
            pltpu.VMEM(block.shape, jnp.bfloat16),
            pltpu.VMEM(sums.shape, jnp.bfloat16),
            pltpu.VMEM((n_col - 1, planes, chunk, LANES), jnp.bfloat16),
            pltpu.VMEM((n_row, planes * part, LANES), jnp.float32),
            pltpu.VMEM((n_row, padded, LANES), jnp.bfloat16),
            pltpu.VMEM((n_row - 1, padded, LANES), jnp.bfloat16),
            pltpu.VMEM((comps * part, LANES), jnp.float32),
            pltpu.VMEM((n_row, comps * part, LANES), jnp.float32),
            pltpu.VMEM((comps, chunk, LANES), jnp.float32),
            pltpu.VMEM((n_col, comps, chunk, LANES), jnp.float32),
            pltpu.VMEM(shapes[2].shape, shapes[2].dtype),
            *[dma((4,))] * 4,
            dma((n_col - 1,)),
            dma((n_col - 1,)),
            dma((n_row - 1,)),
            dma((n_row - 1,)),
            dma((n_row - 1,)),
            dma((n_row - 1,)),
            dma((n_col // 2,)),
            dma((n_col // 2,)),
            dma((n_col // 2,)),
            dma((n_col // 2,)),
        ],
        compiler_params=pltpu.CompilerParams(
            collective_id=1 if halos else 2,
            has_side_effects=True,
            vmem_limit_bytes=48 * 1024 * 1024,
        ),
        cost_estimate=pl.CostEstimate(
            flops=planes * size * LANES * 4, bytes_accessed=8 * 1024 * 1024, transcendentals=0
        ),
        name="exchange",
    )(block, own_grad, *grad_rims, sums, probe_field)
    return new_block, new_probe, tuple(rims)


def local(object_field, probe_field, amplitudes, positions, live_counts):
    frame_size = probe_field.shape[-1]
    tables = chirp_blocks(frame_size)
    rims = first_halos(object_field, frame_size)
    for iteration in range(ITERS):
        planes, rows, columns = object_field.shape
        own_grad, *grad_rims, sums = frame_sums(
            object_field.reshape(planes, rows // SUBLANES, SUBLANES, columns),
            rims,
            probe_field,
            amplitudes,
            positions,
            live_counts,
            tables,
            iteration,
        )
        own_grad = own_grad.reshape(object_field.shape)
        object_field, probe_field, rims = exchange(
            object_field, own_grad, grad_rims, sums, probe_field, iteration < ITERS - 1
        )
    return (object_field, probe_field)


def solution(mesh):
    placed = (
        P(None, "row", "col"),
        P(),
        P(None, ("row", "col"), None, None),
        P(None, None, ("row", "col")),
        P(None, "col", "row"),
    )
    return jax.shard_map(
        local, mesh=mesh, in_specs=placed, out_specs=(P(None, "row", "col"), P()), check_vma=False
    )
```
